256 devices in a mesh: blk: 32 (over z, x_hi, core), rep: 8 (over x_lo, y).
Axes of the slice: x: 4 (x_hi: 2, x_lo: 2; x = x_hi * 2 + x_lo), y: 4, z: 8, core: 2. Of those that a mesh axis runs over, the one named last changes fastest.
Arguments:
- node_features: bfloat16 [65536, 256], P(('blk', 'rep')), may hold values from -6 to 6
- weight: bfloat16 [256, 256], replicated, may hold values from -0.375 to 0.375
- cotangent: bfloat16 [65536, 256], P(('blk', 'rep')), may hold values from -6 to 6
- tile_values: int32 [32, 8, 32, 4, 128, 128], P('blk', 'rep'), may hold values from 0 to 5
- tile_rows: int32 [32, 8, 32, 4], P('blk', 'rep'), may hold values from 0 to 15, as said below
- tile_cols: int32 [32, 8, 32, 4], P('blk', 'rep'), may hold values from 0 to 1, as said below
- tile_count: int32 [32, 8, 32], P('blk', 'rep'), may hold values from 0 to 4, as said below
Outputs:
- activations: bfloat16 [65536, 256], P(('blk', 'rep'))
- feature_grad: bfloat16 [65536, 256], P(('blk', 'rep'))
- weight_grad: float32 [256, 256], replicated
The draws below stay inside these ranges and needn't reach their ends.
Inputs may be any that keep to these rules, and one draw needn't show every extreme that they name: Within one row group, column share and column group, the pairs (tile_rows, tile_cols) of the 4 slots are distinct. `tile_cols`: see tile_rows. `tile_count`: some entry equals 4 in every draw.
All inputs are finite; a program needn't handle non-finite values.
Results may differ from the reference program's by a relative error of at most 0.0064.
Values may be sent and summed in bfloat16 or wider, within the bound.
A program may use at most 64 MiB of HBM per device.

```python
import jax
import jax.numpy as jnp
from jax import lax

F = 256
TILE = 128
NODE_DEV = 256
SLOT = 4
N_NODES = 65536
N_BLK = 32
N_REP = 8


def positions(key):
    row_tiles = NODE_DEV * N_REP // TILE
    col_tiles = NODE_DEV // TILE
    places = row_tiles * col_tiles
    scores = jax.random.randint(key, (N_BLK, N_REP, N_BLK, places), 0, 1 << 16)
    scores = scores * places + jnp.arange(places, dtype=jnp.int32)
    chosen = jnp.argsort(scores, axis=-1, stable=True)[..., :SLOT].astype(jnp.int32)
    return (chosen // col_tiles, chosen % col_tiles)


def draw_tile_rows(key, part):
    shared = positions(key)
    return shared[0].astype(jnp.int32)


def draw_tile_cols(key, part):
    shared = positions(key)
    return shared[1].astype(jnp.int32)


def draw_tile_values(key, part):
    key = jax.random.fold_in(key, 7)
    first_key, second_key = jax.random.split(key)
    full_shape = (N_BLK, N_REP, N_BLK, SLOT, TILE, TILE)
    present = jax.random.randint(first_key, full_shape, 0, 2 * TILE) == 0
    rep_ids = jnp.arange(N_REP, dtype=jnp.int32).reshape(1, N_REP, 1, 1, 1, 1)
    ceiling = 2 + 4 * rep_ids // max(N_REP - 1, 1)
    multiple = jax.random.randint(second_key, full_shape, 1, ceiling)
    return jnp.where(present, multiple, 0).astype(jnp.int32)


def draw_tile_count(key, part):
    key = jax.random.fold_in(key, 11)
    first_key, second_key, third_key = jax.random.split(key, 3)
    full_shape = (N_BLK, N_REP, N_BLK)
    extra = jax.random.randint(first_key, (N_BLK, N_REP, 1), 0, 3)
    base_count = jax.random.randint(second_key, full_shape, 0, SLOT + 1)
    counted = jnp.minimum(base_count + extra, SLOT)
    chosen = jax.random.randint(third_key, (), 0, N_BLK * N_REP * N_BLK)
    flat_ids = jnp.arange(N_BLK * N_REP * N_BLK, dtype=jnp.int32).reshape(full_shape)
    return jnp.where(flat_ids == chosen, SLOT, counted).astype(jnp.int32)


def block_levels(own_key, extent, shards, low, largest):
    gain = 1.0
    for dim, shards_of in shards:
        heights = jax.random.uniform(jax.random.fold_in(jax.random.fold_in(own_key, 6), dim), (shards_of,), jnp.float32, low / len(shards), largest / len(shards))
        gain = gain * jnp.repeat(jnp.exp(heights), extent[dim] // shards_of).reshape((-1,) + (1,) * (len(extent) - 1 - dim))
    return gain


def scatter_about(key, dims, width, bound, shards=(), kind=jnp.bfloat16):
    gain = block_levels(key, dims, shards, -0.22, 0.18) if shards else 1.0
    drawn = jax.random.normal(key, dims, jnp.float32) * width * gain
    return jnp.minimum(jnp.maximum(drawn, -bound), bound).astype(kind)


def setup_inputs(seed: int = 0) -> dict:
    seeds = jax.random.split(jax.random.key(seed), 8)
    node_features = scatter_about(seeds[0], (N_NODES, F), 1.0, 6.0, ((0, 256),))
    weight = scatter_about(seeds[1], (F, F), F ** -0.5, 0.375)
    cotangent = scatter_about(seeds[2], (N_NODES, F), 1.0, 6.0, ((0, 256),))
    tile_values = draw_tile_values(jax.random.fold_in(seeds[7], 71), 0)
    tile_rows = draw_tile_rows(jax.random.fold_in(seeds[7], 71), 0)
    tile_cols = draw_tile_cols(jax.random.fold_in(seeds[7], 71), 0)
    tile_count = draw_tile_count(jax.random.fold_in(seeds[7], 71), 0)
    return {"node_features": node_features, "weight": weight, "cotangent": cotangent, "tile_values": tile_values, "tile_rows": tile_rows, "tile_cols": tile_cols, "tile_count": tile_count}


def silu_slope(pre_act):
    sigmoid_pre = jax.nn.sigmoid(pre_act)
    return sigmoid_pre * (1.0 + pre_act * (1.0 - sigmoid_pre))

def reference(node_features, weight, cotangent, tile_values, tile_rows, tile_cols, tile_count):
    row_tiles = NODE_DEV * N_REP // TILE
    col_tiles = NODE_DEV // TILE
    live_mask = jnp.arange(SLOT, dtype=jnp.int32) < tile_count[..., None]
    feature_grid = node_features.reshape(N_BLK, N_REP, col_tiles, TILE, F)
    rep_ids = jnp.arange(N_REP, dtype=jnp.int32)[:, None, None]
    group_ids = jnp.arange(N_BLK, dtype=jnp.int32)[None, :, None]

    def forward_group(inputs):
        values, rows_here, cols_here, live_here = inputs
        blocks = jnp.where(live_here[..., None, None], values, 0).astype(jnp.float32)
        picked = feature_grid[group_ids, rep_ids, cols_here].astype(jnp.float32)
        product = jnp.einsum('rjsab,rjsbf->rjsaf', blocks, picked, precision=lax.Precision.HIGHEST)
        summed = jnp.zeros((row_tiles, TILE, F), jnp.float32).at[rows_here].add(product)
        degree = jnp.zeros((row_tiles, TILE), jnp.float32).at[rows_here].add(lax.optimization_barrier(jnp.sum(blocks, axis=-1)))
        return (summed.reshape(-1, F), degree.reshape(-1))
    summed, degree = lax.map(forward_group, (tile_values, tile_rows, tile_cols, live_mask))
    summed = summed.reshape(-1, F)
    degree = degree.reshape(-1)
    norm_scale = lax.rsqrt(degree + 1.0)[:, None]
    mixed = ((summed + node_features.astype(jnp.float32)) * norm_scale).astype(jnp.bfloat16)
    pre_act = jnp.dot(mixed, weight, preferred_element_type=jnp.float32)
    activations = jax.nn.silu(pre_act).astype(jnp.bfloat16)
    act_grad = (cotangent.astype(jnp.float32) * silu_slope(pre_act)).astype(jnp.bfloat16)
    weight_grad = jnp.dot(mixed.T, act_grad, preferred_element_type=jnp.float32) * N_NODES ** (-0.5)
    back_proj = jnp.dot(act_grad, weight.T, preferred_element_type=jnp.float32)
    node_grad = (back_proj * norm_scale).astype(jnp.bfloat16)
    grad_grid = node_grad.reshape(N_BLK, row_tiles, TILE, F)

    def backward_group(carry, inputs):
        values, rows_here, cols_here, live_here, grad_here = inputs
        blocks = jnp.where(live_here[..., None, None], values, 0).astype(jnp.float32)
        picked = grad_here[rows_here].astype(jnp.float32)
        product = jnp.einsum('rjsab,rjsaf->rjsbf', blocks, picked, precision=lax.Precision.HIGHEST)
        carry = carry.at[group_ids, rep_ids, cols_here].add(product)
        return (carry, None)
    initial = jnp.zeros((N_BLK, N_REP, col_tiles, TILE, F), jnp.float32)
    spread = lax.scan(backward_group, initial, (tile_values, tile_rows, tile_cols, live_mask, grad_grid))[0]
    feature_grad = (spread.reshape(-1, F) + node_grad.astype(jnp.float32)).astype(jnp.bfloat16)
    return (activations, feature_grad, weight_grad)
```

```python
import jax
import jax.numpy as jnp
from jax import lax
from jax.experimental import pallas as pl
from jax.experimental.pallas import tpu as pltpu
from jax.sharding import PartitionSpec as P

TILE = 128
SLOT = 4


def forward_kernel(rows_ref, cols_ref, count_ref, tiles_ref, feat_ref, sum_ref, deg_ref, kept_ref):
    j = pl.program_id(0)

    @pl.when(j == 0)
    def _():
        sum_ref[...] = jnp.zeros_like(sum_ref)
        deg_ref[...] = jnp.zeros_like(deg_ref)

    for s in range(SLOT):
        live = s < count_ref[j]
        tile = jnp.where(live, tiles_ref[0, s], 0).astype(jnp.float32)
        row = rows_ref[j * SLOT + s]
        col = cols_ref[j * SLOT + s]
        kept = tile.astype(jnp.bfloat16)
        kept_ref[0, s] = kept
        feat = feat_ref[0, pl.ds(pl.multiple_of(col * TILE, TILE), TILE), :]
        sum_ref[row] += jnp.dot(kept, feat, preferred_element_type=jnp.float32)
        deg_ref[row] += jnp.sum(tile, axis=1, keepdims=True)


def backward_kernel(rows_ref, cols_ref, tiles_ref, grad_ref, out_ref):
    j = pl.program_id(0)
    out_ref[...] = jnp.zeros_like(out_ref)
    for s in range(SLOT):
        row = rows_ref[j * SLOT + s]
        col = cols_ref[j * SLOT + s]
        term = lax.dot_general(
            tiles_ref[0, s], grad_ref[row], (((0,), (0,)), ((), ())),
            preferred_element_type=jnp.float32)
        out_ref[0, col] += term


def shards(node_features, weight, cotangent, tile_values, tile_rows, tile_cols, tile_count):
    groups = lax.axis_size("blk")
    replicas = lax.axis_size("rep")
    node_dev, width = node_features.shape
    row_tiles = node_dev * replicas // TILE
    col_tiles = node_dev // TILE
    n_nodes = node_dev * groups * replicas
    rows = tile_rows.reshape(-1)
    cols = tile_cols.reshape(-1)
    count = tile_count.reshape(-1)
    feats = lax.all_gather(node_features, "blk", axis=0, tiled=False)
    summed, degree, kept = pl.pallas_call(
        forward_kernel,
        grid_spec=pltpu.PrefetchScalarGridSpec(
            num_scalar_prefetch=3,
            grid=(groups,),
            in_specs=[
                pl.BlockSpec((1, SLOT, TILE, TILE), lambda j, *_: (j, 0, 0, 0)),
                pl.BlockSpec((1, node_dev, width), lambda j, *_: (j, 0, 0)),
            ],
            out_specs=[
                pl.BlockSpec((row_tiles, TILE, width), lambda j, *_: (0, 0, 0)),
                pl.BlockSpec((row_tiles, TILE, 1), lambda j, *_: (0, 0, 0)),
                pl.BlockSpec((1, SLOT, TILE, TILE), lambda j, *_: (j, 0, 0, 0)),
            ],
        ),
        out_shape=[
            jax.ShapeDtypeStruct((row_tiles, TILE, width), jnp.float32),
            jax.ShapeDtypeStruct((row_tiles, TILE, 1), jnp.float32),
            jax.ShapeDtypeStruct((groups, SLOT, TILE, TILE), jnp.bfloat16),
        ],
        compiler_params=pltpu.CompilerParams(vmem_limit_bytes=32 << 20),
    )(rows, cols, count, tile_values[0, 0], feats)
    summed = lax.psum_scatter(summed.reshape(-1, width), "rep", scatter_dimension=0, tiled=True)
    degree = lax.psum_scatter(degree.reshape(-1), "rep", scatter_dimension=0, tiled=True)
    scale = lax.rsqrt(degree + 1.0)[:, None]
    mixed = ((summed + node_features.astype(jnp.float32)) * scale).astype(jnp.bfloat16)
    pre = jnp.dot(mixed, weight, preferred_element_type=jnp.float32)
    sig = jax.nn.sigmoid(pre)
    activations = (pre * sig).astype(jnp.bfloat16)
    act_grad = (cotangent.astype(jnp.float32) * sig * (1.0 + pre * (1.0 - sig))).astype(jnp.bfloat16)
    weight_part = jnp.einsum("nf,ng->fg", mixed, act_grad, preferred_element_type=jnp.float32)
    weight_grad = lax.psum(weight_part, ("blk", "rep")) * n_nodes ** (-0.5)
    back = jnp.einsum("ng,fg->nf", act_grad, weight, preferred_element_type=jnp.float32)
    node_grad = (back * scale).astype(jnp.bfloat16)
    group_grad = lax.all_gather(node_grad, "rep", axis=0, tiled=True).reshape(row_tiles, TILE, width)
    terms = pl.pallas_call(
        backward_kernel,
        grid_spec=pltpu.PrefetchScalarGridSpec(
            num_scalar_prefetch=2,
            grid=(groups,),
            in_specs=[
                pl.BlockSpec((1, SLOT, TILE, TILE), lambda j, *_: (j, 0, 0, 0)),
                pl.BlockSpec((row_tiles, TILE, width), lambda j, *_: (0, 0, 0)),
            ],
            out_specs=pl.BlockSpec((1, col_tiles, TILE, width), lambda j, *_: (j, 0, 0, 0)),
        ),
        out_shape=jax.ShapeDtypeStruct((groups, col_tiles, TILE, width), jnp.float32),
        compiler_params=pltpu.CompilerParams(vmem_limit_bytes=32 << 20),
    )(rows, cols, kept, group_grad)
    spread = lax.psum_scatter(terms.reshape(-1, width), "blk", scatter_dimension=0, tiled=True)
    feature_grad = (spread + node_grad.astype(jnp.float32)).astype(jnp.bfloat16)
    return activations, feature_grad, weight_grad


def solution(mesh):
    in_specs = (
        P(("blk", "rep"), None),
        P(),
        P(("blk", "rep"), None),
        P("blk", "rep", None, None, None, None),
        P("blk", "rep", None, None),
        P("blk", "rep", None, None),
        P("blk", "rep", None),
    )
    out_specs = (P(("blk", "rep"), None), P(("blk", "rep"), None), P())
    return jax.shard_map(shards, mesh=mesh, in_specs=in_specs, out_specs=out_specs, check_vma=False)
```

```python
import jax
import jax.numpy as jnp
from jax import lax
from jax.experimental import pallas as pl
from jax.experimental.pallas import tpu as pltpu
from jax.sharding import PartitionSpec as P

TILE = 128
SLOT = 4
MESH = pl.DeviceIdType.MESH
F32 = jnp.float32
BF16 = jnp.bfloat16
NZ, NBLK, NREP, NX = 8, 32, 8, 2
POS = NBLK * SLOT


def rem(a, n):
    return lax.rem(a, jnp.int32(n))


def div(a, n):
    return lax.div(a, jnp.int32(n))


def loop(lo, hi, body):
    lax.fori_loop(lo, hi, lambda i, _: (body(i), 0)[1], 0)


def layer_kernel(
    rows_ref, cols_ref, count_ref, rowsv_ref, x_hbm, w_hbm, ct_hbm, tiles_hbm,
    act_ref, fgrad_ref, wgrad_ref,
    xbuf, dbuf, stage, sbuf, degs, idxv, idxs, wbuf, ctbuf,
    rs_src, rs_dst, own, deg_src, deg_dst, mixed, ngt, gt0, gt1,
    ss, sr, zs, zr, xs, xr,
    wp_src, wp_dst, w2s, w2r, w3s, w3r, w4s, w4r, w5s, w5r, w6s, w6r,
    in_sem, tile_sem, idx_sem,
    x_recv, xr_send, xl_send, xs_send, xx_send,
    rs_send, rs_recv, dg_send, dg_recv, g_send, g_recv,
    ss_send, ss_recv, z_send, z_recv, xf_send, xf_recv,
    w1_send, w1_recv, w23_send, w23_recv, w4_send, w4_recv, w5_send, w5_recv, w6_send, w6_recv,
):
    b = lax.axis_index("blk")
    rep = lax.axis_index("rep")
    z, xh, c = div(b, 4), rem(div(b, 2), 2), rem(b, 2)
    gts = (gt0, gt1)

    def blkidx(dz, xq, cq):
        return rem(z + dz + 8, 8) * 4 + rem(xh + xq, 2) * 2 + rem(c + cq, 2)

    def zdev(dz):
        return (blkidx(dz, 0, 0), rep)

    right, left = zdev(1), zdev(-1)
    sibling = (blkidx(0, 0, 1), rep)
    xmate = (blkidx(0, 1, 0), rep)

    def repdev(i):
        return (b, rem(rep + i, NREP))

    def remote(src, dst, send, recv, dev):
        return pltpu.make_async_remote_copy(
            src_ref=src, dst_ref=dst, send_sem=send, recv_sem=recv, device_id=dev, device_id_type=MESH)

    def own_load(h):
        return pltpu.make_async_copy(x_hbm.at[:, pl.ds(h * TILE, TILE)], xbuf.at[h, b], in_sem.at[h])

    def tile_load(p):
        zi, q = div(p, 4), rem(p, 4)
        return pltpu.make_async_copy(tiles_hbm.at[group_at(zi, q)], stage.at[p], tile_sem.at[p])

    def group_at(zi, q):
        odd = rem(zi, 2)
        dz = div(zi, 2) * (1 - 2 * odd) - odd
        return blkidx(dz, div(q, 2), rem(q, 2))

    w_load = pltpu.make_async_copy(w_hbm, wbuf, in_sem.at[2])
    ct_load = pltpu.make_async_copy(ct_hbm, ctbuf, in_sem.at[3])
    idx_copy = pltpu.make_async_copy(idxv, idxs, idx_sem)
    own_load(0).start()
    own_load(1).start()
    loop(0, NBLK, lambda p: tile_load(p).start())
    w_load.start()
    ct_load.start()

    bar = pltpu.get_barrier_semaphore()
    for dev in (sibling, xmate):
        pl.semaphore_signal(bar, inc=1, device_id=dev, device_id_type=MESH)
    loop(1, NZ, lambda i: pl.semaphore_signal(bar, inc=1, device_id=zdev(i), device_id_type=MESH))
    loop(1, NREP, lambda i: pl.semaphore_signal(bar, inc=1, device_id=repdev(i), device_id_type=MESH))

    def rank(i):
        s, j = i & 3, i >> 2
        cj, xj, zj = j & 1, (j >> 1) & 1, j >> 2
        dz = (zj - z + 8) & 7
        zi = jnp.where(dz < 4, 2 * dz, 15 - 2 * dz)
        q = ((xj + xh) & 1) * 2 + ((cj + c) & 1)
        return (zi * 4 + q) * 4 + s

    sub = lax.broadcasted_iota(jnp.int32, (POS, POS), 0)
    lane = lax.broadcasted_iota(jnp.int32, (POS, POS), 1)
    row_l = jnp.broadcast_to(rowsv_ref[...], (POS, POS))
    row_s = jnp.transpose(row_l)
    rank_s, rank_l = rank(sub), rank(lane)
    prev = jnp.max(jnp.where((row_l == row_s) & (rank_s < rank_l), rank_s, -1), axis=0, keepdims=True)
    last = jnp.max(jnp.where(row_s == lane, rank_s, -1), axis=0, keepdims=True)
    idxv[0:1, :] = jnp.where(prev < 0, POS, prev)
    idxv[1:2, :] = jnp.where(last < 0, POS, last)
    idxv[2:8, :] = jnp.zeros((6, POS), jnp.int32)
    idx_copy.start()
    sbuf[POS] = jnp.zeros((TILE, TILE), F32)
    degs[POS] = jnp.zeros((8, TILE), F32)

    own_load(0).wait()
    own_load(1).wait()
    pl.semaphore_wait(bar, 16)

    def f_right(h, j):
        return remote(xbuf.at[h, j], xbuf.at[h, j], xr_send.at[h, j], x_recv.at[h, j], right)

    def f_left(h, j):
        return remote(xbuf.at[h, j], xbuf.at[h, j], xl_send.at[h, j], x_recv.at[h, j], left)

    def f_sib(h, j):
        return remote(xbuf.at[h, j], xbuf.at[h, j], xs_send.at[h, j], x_recv.at[h, j], sibling)

    def f_mate(h):
        return remote(xbuf.at[h, b], xbuf.at[h, b], xx_send.at[h], x_recv.at[h, b], xmate)

    def f_wait(h, j):
        f_sib(h, j).wait_recv()

    def start_own(h):
        f_mate(h).start()
        f_right(h, b).start()
        f_left(h, b).start()
        f_sib(h, b).start()

    start_own(0)
    idx_copy.wait()

    def prep(p, j):
        tile_load(p).wait()
        for s in range(SLOT):
            live = s < count_ref[j]
            col = cols_ref[j * SLOT + s]
            m0 = jnp.where(live & (col == 0), 1.0, 0.0).astype(F32)
            m1 = jnp.where(live & (col == 1), 1.0, 0.0).astype(F32)
            tile = stage[p, s].astype(F32)
            dbuf[j, pl.ds(s * TILE, TILE), 0:TILE] = (tile * m0).astype(BF16)
            dbuf[j, pl.ds(s * TILE, TILE), TILE:2 * TILE] = (tile * m1).astype(BF16)
        ones = jnp.ones((16, 2 * TILE), BF16)
        sums = lax.dot_general(ones, dbuf[j], (((1,), (1,)), ((), ())), preferred_element_type=F32)
        for s in range(SLOT):
            degs[p * SLOT + s] = sums[0:8, s * TILE:(s + 1) * TILE] + degs[idxs[0, j * SLOT + s]]

    def process(h, p):
        zi, q = div(p, 4), rem(p, 4)
        j = group_at(zi, q)
        pl.when(rem(q, 2) == 1)(lambda: f_wait(h, j))
        if h == 0:
            prep(p, j)
        prod = jnp.dot(dbuf[j], xbuf[h, j], preferred_element_type=F32)
        for s in range(SLOT):
            sbuf[p * SLOT + s] = prod[s * TILE:(s + 1) * TILE] + sbuf[idxs[0, j * SLOT + s]]

    def rs_copy(h, r):
        return remote(rs_src.at[h, r], rs_dst.at[h, rep], rs_send.at[h, r], rs_recv.at[h, rep], (b, r))

    def rs_arrival(h, r):
        return remote(rs_src.at[h, r], rs_dst.at[h, r], rs_send.at[h, r], rs_recv.at[h, r], (b, r))

    def dg_copy(r):
        return remote(deg_src.at[r], deg_dst.at[rep], dg_send.at[r], dg_recv.at[rep], (b, r))

    def dg_arrival(r):
        return remote(deg_src.at[r], deg_dst.at[r], dg_send.at[r], dg_recv.at[r], (b, r))

    def forward_half(h):
        far_r, far_l = 4 - h, 3 + h
        jx = blkidx(0, 1, 0)
        f_wait(h, jx)
        f_right(h, jx).start()
        f_left(h, jx).start()
        f_sib(h, jx).start()

        def event(e):
            k, v = 1 + div(e, 4), rem(e, 4)
            sgn, xq = rem(v, 2), div(v, 2)
            j = blkidx(k * (2 * sgn - 1), xq, 0)
            f_wait(h, j)
            pl.when((sgn == 0) & (k < far_r))(lambda: f_right(h, j).start())
            pl.when((sgn == 1) & (k < far_l))(lambda: f_left(h, j).start())
            f_sib(h, j).start()
            p0 = jnp.where(k == 1, v, 4 + (k - 2) * 8 + v * 2)
            loop(p0, p0 + jnp.where(k == 1, 1, 2), lambda p: process(h, p))

        loop(0, 12, event)
        if h == 0:
            start_own(1)

        def far(xq):
            j = blkidx(4, xq, 0)
            f_wait(h, j)
            f_sib(h, j).start()
            loop(20 + xq * 4, 24 + xq * 4, lambda p: process(h, p))

        loop(0, 2, far)
        loop(28, 32, lambda p: process(h, p))

        def chunk(i):
            r = rem(rep + i, NREP)
            for t in range(2):
                rs_src[h, r, pl.ds(t * TILE, TILE)] = sbuf[idxs[1, 2 * r + t]].astype(BF16)
            rs_copy(h, r).start()
            if h == 0:
                for t in range(2):
                    deg_src[r, t] = degs[idxs[1, 2 * r + t]]
                dg_copy(r).start()

        loop(1, NREP, chunk)
        for t in range(2):
            own[h, pl.ds(t * TILE, TILE)] = sbuf[idxs[1, 2 * rep + t]]
            if h == 0:
                deg_src[rep, t] = degs[idxs[1, 2 * rep + t]]

    forward_half(0)
    forward_half(1)

    w_load.wait()
    ct_load.wait()
    loop(1, NREP, lambda i: dg_arrival(rem(rep + i, NREP)).wait_recv())
    deg = deg_src[rep]
    for i in range(1, NREP):
        deg = deg + deg_dst[rem(rep + i, NREP)]
    scale = lax.rsqrt(deg + 1.0)
    scale_row = jnp.concatenate([scale[0, 0:1], scale[1, 0:1]], axis=1)
    scale_col = [jnp.transpose(jnp.broadcast_to(scale[t, 0:1], (TILE, TILE))) for t in range(2)]
    for h in range(2):
        def add(i):
            r = rem(rep + i, NREP)
            rs_arrival(h, r).wait_recv()
            own[h] += rs_dst[h, r].astype(F32)

        loop(1, NREP, add)
        for t in range(2):
            part = own[h, pl.ds(t * TILE, TILE)] + xbuf[h, b, pl.ds(t * TILE, TILE)].astype(F32)
            mixed[pl.ds(t * TILE, TILE), h * TILE:(h + 1) * TILE] = (part * scale_col[t]).astype(BF16)
    pre = jnp.dot(mixed[...], wbuf[...], preferred_element_type=F32)
    sig = 1.0 / (1.0 + jnp.exp(-pre))
    act_ref[...] = (pre * sig).astype(BF16)
    act_grad = (ctbuf[...].astype(F32) * sig * (1.0 + pre * (1.0 - sig))).astype(BF16)

    def g_copy(h, i):
        mine = gts[h].at[pl.ds(2 * rep, 2)]
        return remote(mine, mine, g_send.at[h, i], g_recv.at[h, rep], repdev(i))

    def g_arrival(h, r):
        part = gts[h].at[pl.ds(2 * r, 2)]
        return remote(part, part, g_send.at[h, 0], g_recv.at[h, r], (b, r))

    for h in range(2):
        back = lax.dot_general(
            wbuf[h * TILE:(h + 1) * TILE, :], act_grad, (((1,), (1,)), ((), ())), preferred_element_type=F32)
        grad = (back * scale_row).astype(BF16)
        ngt[h] = grad
        for t in range(2):
            gts[h][2 * rep + t] = grad[:, t * TILE:(t + 1) * TILE]
        loop(1, NREP, lambda i: g_copy(h, i).start())

    def w1_copy(r):
        return remote(wp_src.at[r], wp_dst.at[rep], w1_send.at[r], w1_recv.at[rep], (b, r))

    def w1_arrival(r):
        return remote(wp_src.at[r], wp_dst.at[r], w1_send.at[r], w1_recv.at[r], (b, r))

    w2_copy = remote(w2s, w2r, w23_send.at[0], w23_recv.at[0], sibling)
    w3_copy = remote(w3s, w3r, w23_send.at[1], w23_recv.at[1], xmate)

    def w4_copy(i):
        zz = rem(z + i, NZ)
        return remote(w4s.at[zz], w4r.at[z], w4_send.at[zz], w4_recv.at[z], zdev(i))

    def w4_arrival(zz):
        return remote(w4s.at[zz], w4r.at[zz], w4_send.at[zz], w4_recv.at[zz], right)

    def w5_copy(i):
        return remote(w5s, w5r.at[z], w5_send.at[i], w5_recv.at[z], zdev(i))

    def w5_arrival(zz):
        return remote(w5s, w5r.at[zz], w5_send.at[0], w5_recv.at[zz], right)

    def w6_copy(i):
        return remote(w6s, w6r.at[rep], w6_send.at[i], w6_recv.at[rep], repdev(i))

    def w6_arrival(r):
        return remote(w6s, w6r.at[r], w6_send.at[0], w6_recv.at[r], (b, r))

    part = lax.dot_general(mixed[...], act_grad, (((0,), (0,)), ((), ())), preferred_element_type=F32)
    for r in range(NREP):
        wp_src[r] = part[r * 32:(r + 1) * 32]
    loop(1, NREP, lambda i: w1_copy(rem(rep + i, NREP)).start())

    def w_step2():
        loop(1, NREP, lambda i: w1_arrival(rem(rep + i, NREP)).wait_recv())
        wp_dst[rep] = wp_src[rep]
        w2s[...] = sum(wp_dst[r] for r in range(NREP))
        w2_copy.start()

    def w_step3():
        w2_copy.wait_recv()
        w3s[...] = w2s[...] + w2r[...]
        w3_copy.start()

    def w_step4():
        w3_copy.wait_recv()
        both = w3s[...] + w3r[...]
        for k in range(NZ):
            w4s[k] = both[(k // 2) * 8:(k // 2) * 8 + 8, (k % 2) * TILE:(k % 2) * TILE + TILE]
        loop(1, NZ, lambda i: w4_copy(i).start())

    def w_step5():
        loop(1, NZ, lambda i: w4_arrival(rem(z + i, NZ)).wait_recv())
        w4r[z] = w4s[z]
        w5s[...] = sum(w4r[k] for k in range(NZ))
        loop(1, NZ, lambda i: w5_copy(i).start())

    def w_step6():
        loop(1, NZ, lambda i: w5_arrival(rem(z + i, NZ)).wait_recv())
        w5r[z] = w5s[...]
        for k in range(NZ):
            w6s[(k // 2) * 8:(k // 2) * 8 + 8, (k % 2) * TILE:(k % 2) * TILE + TILE] = w5r[k]
        loop(1, NREP, lambda i: w6_copy(i).start())

    def w_step7():
        loop(1, NREP, lambda i: w6_arrival(rem(rep + i, NREP)).wait_recv())
        w6r[rep] = w6s[...]
        for r in range(NREP):
            wgrad_ref[r * 32:(r + 1) * 32] = w6r[r] * (NBLK * NREP * 2 * TILE) ** -0.5

    def out_t(h, j):
        left_side = jnp.concatenate([gts[h][rows_ref[j * SLOT + s]] for s in range(SLOT)], axis=1)
        return jnp.dot(left_side, dbuf[j], preferred_element_type=F32)

    def sib_copy(h, k):
        return remote(ss.at[h, k], sr.at[h, k], ss_send.at[h, k], ss_recv.at[h, k], sibling)

    def z_copy(h, d, m, xq):
        i = (d * 4 + m - 1) * 2 + xq
        dev = (jnp.where(d == 0, right[0], left[0]), rep)
        return remote(zs.at[h, i], zr.at[h, i], z_send.at[h, i], z_recv.at[h, i], dev)

    def z_arrival(h, d, m, xq):
        i = (d * 4 + m) * 2 + xq
        return remote(zs.at[h, i], zr.at[h, i], z_send.at[h, i], z_recv.at[h, i], right)

    def z_value(h, d, m, xq):
        return zr[h, (d * 4 + m) * 2 + xq].astype(F32)

    def x_copy(h):
        return remote(xs.at[h], xr.at[h], xf_send.at[h], xf_recv.at[h], xmate)

    def sib_term(h, d, m, xq):
        dz = m * (1 - 2 * d)
        k = rem(dz + 8, 8) * 2 + xq
        ss[h, k] = out_t(h, blkidx(dz, xq, 1)).astype(BF16)
        sib_copy(h, k).start()

    def own_term(h, d, m, xq, first):
        dz = m * (1 - 2 * d)
        k = rem(dz + 8, 8) * 2 + xq
        value = out_t(h, blkidx(dz, xq, 0))
        sib_copy(h, k).wait_recv()
        value = value + sr[h, k].astype(F32)
        if not first:
            return value, k
        zs[h, (d * 4 + m - 1) * 2 + xq] = value.astype(BF16)
        z_copy(h, d, m, xq).start()

    def pass_on(h, d, m, xq):
        value, _ = own_term(h, d, m, xq, False)
        i = (d * 4 + m) * 2 + xq
        z_arrival(h, d, m, xq).wait_recv()
        zs[h, i - 2] = (value + zr[h, i].astype(F32)).astype(BF16)
        z_copy(h, d, m, xq).start()

    def backward_open(h):
        long, short = h, 1 - h
        loop(1, NREP, lambda i: g_arrival(h, rem(rep + i, NREP)).wait_recv())
        loop(0, 2, lambda q: sib_term(h, long, 4, q))
        loop(0, 2, lambda q: sib_term(h, short, 3, q))
        loop(0, 2, lambda q: own_term(h, long, 4, q, True))
        loop(0, 2, lambda q: sib_term(h, long, 3, q))
        loop(0, 2, lambda q: own_term(h, short, 3, q, True))

    def backward_mid(h):
        long, short = h, 1 - h

        def third(q):
            sib_term(h, 0, 2, q)
            sib_term(h, 1, 2, q)
            pass_on(h, long, 3, q)

        loop(0, 2, third)

        def second(e):
            d, q = rem(e, 2), div(e, 2)
            sib_term(h, d, 1, q)
            pass_on(h, d, 2, q)

        loop(0, 4, second)
        loop(0, 2, lambda q: sib_term(h, 0, 0, q))
        loop(0, 4, lambda e: pass_on(h, rem(e, 2), 1, div(e, 2)))

    def settled(h, xq):
        value, _ = own_term(h, 0, 0, xq, False)
        z_arrival(h, 0, 0, xq).wait_recv()
        z_arrival(h, 1, 0, xq).wait_recv()
        return value + z_value(h, 0, 0, xq) + z_value(h, 1, 0, xq)

    def to_mate(h):
        xs[h] = settled(h, 1).astype(BF16)
        x_copy(h).start()

    def finish(h):
        value = settled(h, 0)
        x_copy(h).wait_recv()
        value = value + xr[h].astype(F32) + ngt[h].astype(F32)
        fgrad_ref[:, h * TILE:(h + 1) * TILE] = jnp.transpose(value).astype(BF16)

    backward_open(0)
    w_step2()
    backward_mid(0)
    w_step3()
    backward_open(1)
    w_step4()
    to_mate(0)
    w_step5()
    backward_mid(1)
    w_step6()
    finish(0)
    to_mate(1)
    w_step7()
    finish(1)

    for h in range(2):
        far_r, far_l = 4 - h, 3 + h
        f_mate(h).wait_send()

        def drain_f(e):
            k, xq = div(e, 2), rem(e, 2)
            f_right(h, blkidx(-k, xq, 0)).wait_send()
            f_left(h, blkidx(k, xq, 0)).wait_send()

        loop(0, 6, drain_f)

        def drain_long(xq):
            if h == 0:
                f_right(h, blkidx(-3, xq, 0)).wait_send()
            else:
                f_left(h, blkidx(3, xq, 0)).wait_send()
            z_copy(h, h, 4, xq).wait_send()

        loop(0, 2, drain_long)

        def drain_s(e):
            f_sib(h, blkidx(div(e, 2), rem(e, 2), 0)).wait_send()
            sib_copy(h, e).wait_send()

        loop(0, 16, drain_s)

        def drain_z(e):
            z_copy(h, rem(e, 2), 1 + div(e, 4), rem(div(e, 2), 2)).wait_send()

        loop(0, 12, drain_z)
        x_copy(h).wait_send()

        def drain_rep(i):
            rs_copy(h, rem(rep + i, NREP)).wait_send()
            g_copy(h, i).wait_send()

        loop(1, NREP, drain_rep)

    def drain_w(i):
        r = rem(rep + i, NREP)
        dg_copy(r).wait_send()
        w1_copy(r).wait_send()
        w4_copy(i).wait_send()
        w5_copy(i).wait_send()
        w6_copy(i).wait_send()

    loop(1, NREP, drain_w)
    w2_copy.wait_send()
    w3_copy.wait_send()


def shards(node_features, weight, cotangent, tile_values, tile_rows, tile_cols, tile_count):
    half, width = TILE, 2 * TILE
    dma = pltpu.SemaphoreType.DMA
    vmem = pltpu.VMEM
    smem_spec = pl.BlockSpec(memory_space=pltpu.SMEM)
    vmem_spec = pl.BlockSpec(memory_space=pltpu.VMEM)
    any_spec = pl.BlockSpec(memory_space=pl.ANY)
    return pl.pallas_call(
        layer_kernel,
        out_shape=[
            jax.ShapeDtypeStruct((width, width), BF16),
            jax.ShapeDtypeStruct((width, width), BF16),
            jax.ShapeDtypeStruct((width, width), F32),
        ],
        in_specs=[smem_spec] * 3 + [vmem_spec] + [any_spec] * 4,
        out_specs=[vmem_spec] * 3,
        scratch_shapes=[
            vmem((2, NBLK, width, half), BF16),
            vmem((NBLK, SLOT * TILE, width), BF16),
            vmem((NBLK, SLOT, TILE, TILE), jnp.int32),
            vmem((POS + 1, TILE, TILE), F32),
            vmem((POS + 1, 8, TILE), F32),
            vmem((8, POS), jnp.int32),
            pltpu.SMEM((8, POS), jnp.int32),
            vmem((width, width), BF16),
            vmem((width, width), BF16),
            vmem((2, NREP, width, half), BF16),
            vmem((2, NREP, width, half), BF16),
            vmem((2, width, half), F32),
            vmem((NREP, 2, 8, TILE), F32),
            vmem((NREP, 2, 8, TILE), F32),
            vmem((width, width), BF16),
            vmem((2, half, width), BF16),
            vmem((2 * NREP, half, TILE), BF16),
            vmem((2 * NREP, half, TILE), BF16),
            vmem((2, 16, half, width), BF16),
            vmem((2, 16, half, width), BF16),
            vmem((2, 16, half, width), BF16),
            vmem((2, 16, half, width), BF16),
            vmem((2, half, width), BF16),
            vmem((2, half, width), BF16),
            vmem((NREP, 32, width), F32),
            vmem((NREP, 32, width), F32),
            vmem((32, width), F32),
            vmem((32, width), F32),
            vmem((32, width), F32),
            vmem((32, width), F32),
            vmem((NZ, 8, TILE), F32),
            vmem((NZ, 8, TILE), F32),
            vmem((8, TILE), F32),
            vmem((NZ, 8, TILE), F32),
            vmem((32, width), F32),
            vmem((NREP, 32, width), F32),
            dma((4,)), dma((NBLK,)), dma,
            dma((2, NBLK)), dma((2, NBLK)), dma((2, NBLK)), dma((2, NBLK)), dma((2,)),
            dma((2, NREP)), dma((2, NREP)), dma((NREP,)), dma((NREP,)), dma((2, NREP)), dma((2, NREP)),
            dma((2, 16)), dma((2, 16)), dma((2, 16)), dma((2, 16)), dma((2,)), dma((2,)),
            dma((NREP,)), dma((NREP,)), dma((2,)), dma((2,)), dma((NZ,)), dma((NZ,)), dma((NZ,)), dma((NZ,)),
            dma((NREP,)), dma((NREP,)),
        ],
        compiler_params=pltpu.CompilerParams(
            collective_id=0, has_side_effects=True, vmem_limit_bytes=56 << 20),
        cost_estimate=pl.CostEstimate(flops=4 << 30, bytes_accessed=9 << 20, transcendentals=1 << 16),
        name="graph_layer",
    )(
        tile_rows.reshape(-1), tile_cols.reshape(-1), tile_count.reshape(-1), tile_rows.reshape(1, -1),
        node_features, weight, cotangent, tile_values[0, 0],
    )


def solution(mesh):
    in_specs = (
        P(("blk", "rep"), None),
        P(),
        P(("blk", "rep"), None),
        P("blk", "rep", None, None, None, None),
        P("blk", "rep", None, None),
        P("blk", "rep", None, None),
        P("blk", "rep", None),
    )
    out_specs = (P(("blk", "rep"), None), P(("blk", "rep"), None), P())
    return jax.shard_map(shards, mesh=mesh, in_specs=in_specs, out_specs=out_specs, check_vma=False)
```

```python
import jax
import jax.numpy as jnp
from jax import lax
from jax.experimental import pallas as pl
from jax.experimental.pallas import tpu as pltpu
from jax.sharding import PartitionSpec as P

TILE = 128
SLOT = 4
MESH = pl.DeviceIdType.MESH
F32 = jnp.float32
BF16 = jnp.bfloat16
NZ, NBLK, NREP, NX = 8, 32, 8, 2
POS = NBLK * SLOT


def rem(a, n):
    return lax.rem(a, jnp.int32(n))


def div(a, n):
    return lax.div(a, jnp.int32(n))


def loop(lo, hi, body):
    lax.fori_loop(lo, hi, lambda i, _: (body(i), 0)[1], 0)


def layer_kernel(
    rows_ref, cols_ref, count_ref, rowsv_ref, x_hbm, w_hbm, ct_hbm, tiles_hbm,
    act_ref, fgrad_ref, wgrad_ref,
    xbuf, dbuf, stage, sbuf, degs, idxv, idxs, wbuf, ctbuf,
    rs_src, rs_dst, own, deg_src, deg_dst, mixed, ngt, gt0, gt1,
    ss, sr, zs, zr, xs, xr,
    wp_src, wp_dst, w2s, w2r, w3s, w3r, w4s, w4r, w5s, w5r, w6s, w6r,
    in_sem, tile_sem, idx_sem,
    x_recv, xr_send, xl_send, xs_send, xx_send,
    rs_send, rs_recv, dg_send, dg_recv, g_send, g_recv,
    ss_send, ss_recv, z_send, z_recv, xf_send, xf_recv,
    w1_send, w1_recv, w23_send, w23_recv, w4_send, w4_recv, w5_send, w5_recv, w6_send, w6_recv,
):
    b = lax.axis_index("blk")
    rep = lax.axis_index("rep")
    z, xh, c = div(b, 4), rem(div(b, 2), 2), rem(b, 2)
    gts = (gt0, gt1)

    def blkidx(dz, xq, cq):
        return rem(z + dz + 8, 8) * 4 + rem(xh + xq, 2) * 2 + rem(c + cq, 2)

    def zdev(dz):
        return (blkidx(dz, 0, 0), rep)

    right, left = zdev(1), zdev(-1)
    sibling = (blkidx(0, 0, 1), rep)
    xmate = (blkidx(0, 1, 0), rep)

    def repdev(i):
        return (b, rem(rep + i, NREP))

    def remote(src, dst, send, recv, dev):
        return pltpu.make_async_remote_copy(
            src_ref=src, dst_ref=dst, send_sem=send, recv_sem=recv, device_id=dev, device_id_type=MESH)

    def own_load(h):
        return pltpu.make_async_copy(x_hbm.at[:, pl.ds(h * TILE, TILE)], xbuf.at[h, b], in_sem.at[h])

    def tile_load(p):
        zi, q = div(p, 4), rem(p, 4)
        return pltpu.make_async_copy(tiles_hbm.at[group_at(zi, q)], stage.at[p], tile_sem.at[p])

    def group_at(zi, q):
        odd = rem(zi, 2)
        dz = div(zi, 2) * (1 - 2 * odd) - odd
        return blkidx(dz, div(q, 2), rem(q, 2))

    w_load = pltpu.make_async_copy(w_hbm, wbuf, in_sem.at[2])
    ct_load = pltpu.make_async_copy(ct_hbm, ctbuf, in_sem.at[3])
    idx_copy = pltpu.make_async_copy(idxv, idxs, idx_sem)
    own_load(0).start()
    own_load(1).start()
    loop(0, NBLK, lambda p: tile_load(p).start())
    w_load.start()
    ct_load.start()

    bar = pltpu.get_barrier_semaphore()
    for dev in (sibling, xmate):
        pl.semaphore_signal(bar, inc=1, device_id=dev, device_id_type=MESH)
    loop(1, NZ, lambda i: pl.semaphore_signal(bar, inc=1, device_id=zdev(i), device_id_type=MESH))
    loop(1, NREP, lambda i: pl.semaphore_signal(bar, inc=1, device_id=repdev(i), device_id_type=MESH))

    def first_pos(j):
        cj, xj, zj = j & 1, (j >> 1) & 1, j >> 2
        dz = (zj - z + 8) & 7
        zi = jnp.where(dz < 4, 2 * dz, 15 - 2 * dz)
        q = ((xj + xh) & 1) * 2 + ((cj + c) & 1)
        return (zi * 4 + q) * SLOT

    idxv[...] = jnp.zeros((8, TILE), jnp.int32)
    idxv[0:SLOT, 0:NBLK] = rowsv_ref[...]
    group = lax.broadcasted_iota(jnp.int32, (NBLK, TILE), 0)
    lane = lax.broadcasted_iota(jnp.int32, (NBLK, TILE), 1)
    group_pos, lane_pos = first_pos(group), first_pos(lane & (NBLK - 1))
    row_l = [jnp.broadcast_to(idxv[s:s + 1, :], (TILE, TILE)) for s in range(SLOT)]
    row_s = [jnp.transpose(row)[0:NBLK] for row in row_l]
    last = jnp.full((NBLK, TILE), -1, jnp.int32)
    for t in range(SLOT):
        last = jnp.maximum(last, jnp.where(row_s[t] == lane, group_pos + t, -1))
    last = jnp.max(last, axis=0, keepdims=True)
    for s in range(SLOT):
        prev = jnp.full((NBLK, TILE), -1, jnp.int32)
        for t in range(SLOT):
            before = (row_s[t] == row_l[s][0:NBLK]) & (group_pos + t < lane_pos + s)
            prev = jnp.maximum(prev, jnp.where(before, group_pos + t, -1))
        prev = jnp.max(prev, axis=0, keepdims=True)
        idxv[s:s + 1, :] = jnp.where(prev < 0, POS, prev)
    idxv[SLOT:SLOT + 1, :] = jnp.where(last < 0, POS, last)
    idx_copy.start()
    for h in range(2):
        sbuf[h, POS] = jnp.zeros((TILE, TILE), F32)
    degs[POS] = jnp.zeros((8, TILE), F32)

    own_load(0).wait()
    own_load(1).wait()
    pl.semaphore_wait(bar, 16)

    def f_right(h, j):
        return remote(xbuf.at[h, j], xbuf.at[h, j], xr_send.at[h, j], x_recv.at[h, j], right)

    def f_left(h, j):
        return remote(xbuf.at[h, j], xbuf.at[h, j], xl_send.at[h, j], x_recv.at[h, j], left)

    def f_sib(h, j):
        return remote(xbuf.at[h, j], xbuf.at[h, j], xs_send.at[h, j], x_recv.at[h, j], sibling)

    def f_mate(h):
        return remote(xbuf.at[h, b], xbuf.at[h, b], xx_send.at[h], x_recv.at[h, b], xmate)

    def f_wait(h, j):
        f_sib(h, j).wait_recv()

    def start_own(h):
        f_mate(h).start()
        f_right(h, b).start()
        f_left(h, b).start()
        f_sib(h, b).start()

    start_own(0)
    start_own(1)
    idx_copy.wait()

    def prep(p, j):
        tile_load(p).wait()
        for s in range(SLOT):
            live = s < count_ref[j]
            col = cols_ref[s, j]
            m0 = jnp.where(live & (col == 0), 1.0, 0.0).astype(F32)
            m1 = jnp.where(live & (col == 1), 1.0, 0.0).astype(F32)
            tile = stage[p, s].astype(F32)
            dbuf[j, pl.ds(s * TILE, TILE), 0:TILE] = (tile * m0).astype(BF16)
            dbuf[j, pl.ds(s * TILE, TILE), TILE:2 * TILE] = (tile * m1).astype(BF16)
        ones = jnp.ones((16, 2 * TILE), BF16)
        sums = lax.dot_general(ones, dbuf[j], (((1,), (1,)), ((), ())), preferred_element_type=F32)
        for s in range(SLOT):
            degs[p * SLOT + s] = sums[0:8, s * TILE:(s + 1) * TILE] + degs[idxs[s, j]]

    def process(h, p):
        zi, q = div(p, 4), rem(p, 4)
        j = group_at(zi, q)
        pl.when(rem(q, 2) == 1)(lambda: f_wait(h, j))
        if h == 0:
            prep(p, j)
        prod = jnp.dot(dbuf[j], xbuf[h, j], preferred_element_type=F32)
        for s in range(SLOT):
            sbuf[h, p * SLOT + s] = prod[s * TILE:(s + 1) * TILE] + sbuf[h, idxs[s, j]]

    def rs_copy(h, r):
        return remote(rs_src.at[h, r], rs_dst.at[h, rep], rs_send.at[h, r], rs_recv.at[h, rep], (b, r))

    def rs_arrival(h, r):
        return remote(rs_src.at[h, r], rs_dst.at[h, r], rs_send.at[h, r], rs_recv.at[h, r], (b, r))

    def dg_copy(r):
        return remote(deg_src.at[r], deg_dst.at[rep], dg_send.at[r], dg_recv.at[rep], (b, r))

    def dg_arrival(r):
        return remote(deg_src.at[r], deg_dst.at[r], dg_send.at[r], dg_recv.at[r], (b, r))

    def forward_open(h):
        jx = blkidx(0, 1, 0)
        f_wait(h, jx)
        f_right(h, jx).start()
        f_left(h, jx).start()
        f_sib(h, jx).start()

    def forward_step(h, k):
        far_r, far_l = 4 - h, 3 + h

        def event(v):
            sgn, xq = rem(v, 2), div(v, 2)
            j = blkidx(k * (2 * sgn - 1), xq, 0)
            f_wait(h, j)
            if k < far_r:
                pl.when(sgn == 0)(lambda: f_right(h, j).start())
            if k < far_l:
                pl.when(sgn == 1)(lambda: f_left(h, j).start())
            f_sib(h, j).start()
            n = 1 if k == 1 else 2
            p0 = v if k == 1 else 4 + (k - 2) * 8 + v * 2
            loop(p0, p0 + n, lambda p: process(h, p))

        loop(0, 4, event)

    def forward_close(h):
        def far(xq):
            j = blkidx(4, xq, 0)
            f_wait(h, j)
            f_sib(h, j).start()
            loop(20 + xq * 4, 24 + xq * 4, lambda p: process(h, p))

        loop(0, 2, far)
        loop(28, 32, lambda p: process(h, p))

        def chunk(i):
            r = rem(rep + i, NREP)
            for t in range(2):
                rs_src[h, r, pl.ds(t * TILE, TILE)] = sbuf[h, idxs[SLOT, 2 * r + t]].astype(BF16)
            rs_copy(h, r).start()
            if h == 0:
                for t in range(2):
                    deg_src[r, t] = degs[idxs[SLOT, 2 * r + t]]
                dg_copy(r).start()

        loop(1, NREP, chunk)
        for t in range(2):
            own[h, pl.ds(t * TILE, TILE)] = sbuf[h, idxs[SLOT, 2 * rep + t]]
            if h == 0:
                deg_src[rep, t] = degs[idxs[SLOT, 2 * rep + t]]

    forward_open(0)
    forward_open(1)
    for k in range(1, 4):
        forward_step(0, k)
        if k > 1:
            forward_step(1, k - 1)
    forward_close(0)
    forward_step(1, 3)
    forward_close(1)

    w_load.wait()
    ct_load.wait()
    loop(1, NREP, lambda i: dg_arrival(rem(rep + i, NREP)).wait_recv())
    deg = deg_src[rep]
    for i in range(1, NREP):
        deg = deg + deg_dst[rem(rep + i, NREP)]
    scale = lax.rsqrt(deg + 1.0)
    scale_row = jnp.concatenate([scale[0, 0:1], scale[1, 0:1]], axis=1)
    scale_col = [jnp.transpose(jnp.broadcast_to(scale[t, 0:1], (TILE, TILE))) for t in range(2)]
    for h in range(2):
        def add(i):
            r = rem(rep + i, NREP)
            rs_arrival(h, r).wait_recv()
            own[h] += rs_dst[h, r].astype(F32)

        loop(1, NREP, add)
        for t in range(2):
            part = own[h, pl.ds(t * TILE, TILE)] + xbuf[h, b, pl.ds(t * TILE, TILE)].astype(F32)
            mixed[pl.ds(t * TILE, TILE), h * TILE:(h + 1) * TILE] = (part * scale_col[t]).astype(BF16)
    pre = jnp.dot(mixed[...], wbuf[...], preferred_element_type=F32)
    sig = 1.0 / (1.0 + jnp.exp(-pre))
    act_ref[...] = (pre * sig).astype(BF16)
    act_grad = (ctbuf[...].astype(F32) * sig * (1.0 + pre * (1.0 - sig))).astype(BF16)

    def g_copy(h, i):
        mine = gts[h].at[pl.ds(2 * rep, 2)]
        return remote(mine, mine, g_send.at[h, i], g_recv.at[h, rep], repdev(i))

    def g_arrival(h, r):
        part = gts[h].at[pl.ds(2 * r, 2)]
        return remote(part, part, g_send.at[h, 0], g_recv.at[h, r], (b, r))

    for h in range(2):
        back = lax.dot_general(
            wbuf[h * TILE:(h + 1) * TILE, :], act_grad, (((1,), (1,)), ((), ())), preferred_element_type=F32)
        grad = (back * scale_row).astype(BF16)
        ngt[h] = grad
        for t in range(2):
            gts[h][2 * rep + t] = grad[:, t * TILE:(t + 1) * TILE]
        loop(1, NREP, lambda i: g_copy(h, i).start())

    def w1_copy(r):
        return remote(wp_src.at[r], wp_dst.at[rep], w1_send.at[r], w1_recv.at[rep], (b, r))

    def w1_arrival(r):
        return remote(wp_src.at[r], wp_dst.at[r], w1_send.at[r], w1_recv.at[r], (b, r))

    w2_copy = remote(w2s, w2r, w23_send.at[0], w23_recv.at[0], sibling)
    w3_copy = remote(w3s, w3r, w23_send.at[1], w23_recv.at[1], xmate)

    def w4_copy(i):
        zz = rem(z + i, NZ)
        return remote(w4s.at[zz], w4r.at[z], w4_send.at[zz], w4_recv.at[z], zdev(i))

    def w4_arrival(zz):
        return remote(w4s.at[zz], w4r.at[zz], w4_send.at[zz], w4_recv.at[zz], right)

    def w5_copy(i):
        return remote(w5s, w5r.at[z], w5_send.at[i], w5_recv.at[z], zdev(i))

    def w5_arrival(zz):
        return remote(w5s, w5r.at[zz], w5_send.at[0], w5_recv.at[zz], right)

    def w6_copy(i):
        return remote(w6s, w6r.at[rep], w6_send.at[i], w6_recv.at[rep], repdev(i))

    def w6_arrival(r):
        return remote(w6s, w6r.at[r], w6_send.at[0], w6_recv.at[r], (b, r))

    part = lax.dot_general(mixed[...], act_grad, (((0,), (0,)), ((), ())), preferred_element_type=F32)
    for r in range(NREP):
        wp_src[r] = part[r * 32:(r + 1) * 32]
    loop(1, NREP, lambda i: w1_copy(rem(rep + i, NREP)).start())

    def w_step2():
        loop(1, NREP, lambda i: w1_arrival(rem(rep + i, NREP)).wait_recv())
        wp_dst[rep] = wp_src[rep]
        w2s[...] = sum(wp_dst[r] for r in range(NREP))
        w2_copy.start()

    def w_step3():
        w2_copy.wait_recv()
        w3s[...] = w2s[...] + w2r[...]
        w3_copy.start()

    def w_step4():
        w3_copy.wait_recv()
        both = w3s[...] + w3r[...]
        for k in range(NZ):
            w4s[k] = both[(k // 2) * 8:(k // 2) * 8 + 8, (k % 2) * TILE:(k % 2) * TILE + TILE]
        loop(1, NZ, lambda i: w4_copy(i).start())

    def w_step5():
        loop(1, NZ, lambda i: w4_arrival(rem(z + i, NZ)).wait_recv())
        w4r[z] = w4s[z]
        w5s[...] = sum(w4r[k] for k in range(NZ))
        loop(1, NZ, lambda i: w5_copy(i).start())

    def w_step6():
        loop(1, NZ, lambda i: w5_arrival(rem(z + i, NZ)).wait_recv())
        w5r[z] = w5s[...]
        for k in range(NZ):
            w6s[(k // 2) * 8:(k // 2) * 8 + 8, (k % 2) * TILE:(k % 2) * TILE + TILE] = w5r[k]
        loop(1, NREP, lambda i: w6_copy(i).start())

    def w_step7():
        loop(1, NREP, lambda i: w6_arrival(rem(rep + i, NREP)).wait_recv())
        w6r[rep] = w6s[...]
        for r in range(NREP):
            wgrad_ref[r * 32:(r + 1) * 32] = w6r[r] * (NBLK * NREP * 2 * TILE) ** -0.5

    def out_t(h, j):
        left_side = jnp.concatenate([gts[h][rows_ref[s, j]] for s in range(SLOT)], axis=1)
        return jnp.dot(left_side, dbuf[j], preferred_element_type=F32)

    def sib_copy(h, k):
        return remote(ss.at[h, k], sr.at[h, k], ss_send.at[h, k], ss_recv.at[h, k], sibling)

    def z_copy(h, d, m, xq):
        i = (d * 4 + m - 1) * 2 + xq
        dev = (jnp.where(d == 0, right[0], left[0]), rep)
        return remote(zs.at[h, i], zr.at[h, i], z_send.at[h, i], z_recv.at[h, i], dev)

    def z_arrival(h, d, m, xq):
        i = (d * 4 + m) * 2 + xq
        return remote(zs.at[h, i], zr.at[h, i], z_send.at[h, i], z_recv.at[h, i], right)

    def z_value(h, d, m, xq):
        return zr[h, (d * 4 + m) * 2 + xq].astype(F32)

    def x_copy(h):
        return remote(xs.at[h], xr.at[h], xf_send.at[h], xf_recv.at[h], xmate)

    def sib_term(h, d, m, xq):
        dz = m * (1 - 2 * d)
        k = rem(dz + 8, 8) * 2 + xq
        ss[h, k] = out_t(h, blkidx(dz, xq, 1)).astype(BF16)
        sib_copy(h, k).start()

    def own_term(h, d, m, xq, first):
        dz = m * (1 - 2 * d)
        k = rem(dz + 8, 8) * 2 + xq
        value = out_t(h, blkidx(dz, xq, 0))
        sib_copy(h, k).wait_recv()
        value = value + sr[h, k].astype(F32)
        if not first:
            return value, k
        zs[h, (d * 4 + m - 1) * 2 + xq] = value.astype(BF16)
        z_copy(h, d, m, xq).start()

    def pass_on(h, d, m, xq):
        value, _ = own_term(h, d, m, xq, False)
        i = (d * 4 + m) * 2 + xq
        z_arrival(h, d, m, xq).wait_recv()
        zs[h, i - 2] = (value + zr[h, i].astype(F32)).astype(BF16)
        z_copy(h, d, m, xq).start()

    def backward_open(h):
        long, short = h, 1 - h
        loop(1, NREP, lambda i: g_arrival(h, rem(rep + i, NREP)).wait_recv())
        loop(0, 2, lambda q: sib_term(h, long, 4, q))
        loop(0, 2, lambda q: sib_term(h, short, 3, q))
        loop(0, 2, lambda q: own_term(h, long, 4, q, True))
        loop(0, 2, lambda q: sib_term(h, long, 3, q))
        loop(0, 2, lambda q: own_term(h, short, 3, q, True))

    def backward_third(h):
        def third(q):
            sib_term(h, 0, 2, q)
            sib_term(h, 1, 2, q)
            pass_on(h, h, 3, q)

        loop(0, 2, third)

    def backward_second(h):
        def second(e):
            d, q = rem(e, 2), div(e, 2)
            sib_term(h, d, 1, q)
            pass_on(h, d, 2, q)

        loop(0, 4, second)

    def backward_first(h):
        loop(0, 2, lambda q: sib_term(h, 0, 0, q))
        loop(0, 4, lambda e: pass_on(h, rem(e, 2), 1, div(e, 2)))

    def settled(h, xq):
        value, _ = own_term(h, 0, 0, xq, False)
        z_arrival(h, 0, 0, xq).wait_recv()
        z_arrival(h, 1, 0, xq).wait_recv()
        return value + z_value(h, 0, 0, xq) + z_value(h, 1, 0, xq)

    def to_mate(h):
        xs[h] = settled(h, 1).astype(BF16)
        x_copy(h).start()

    def finish(h):
        value = settled(h, 0)
        x_copy(h).wait_recv()
        value = value + xr[h].astype(F32) + ngt[h].astype(F32)
        fgrad_ref[:, h * TILE:(h + 1) * TILE] = jnp.transpose(value).astype(BF16)

    backward_open(0)
    w_step2()
    backward_open(1)
    w_step3()
    backward_third(0)
    backward_third(1)
    w_step4()
    backward_second(0)
    backward_second(1)
    w_step5()
    backward_first(0)
    backward_first(1)
    w_step6()
    to_mate(0)
    to_mate(1)
    w_step7()
    finish(0)
    finish(1)

    for h in range(2):
        far_r, far_l = 4 - h, 3 + h
        f_mate(h).wait_send()

        def drain_f(e):
            k, xq = div(e, 2), rem(e, 2)
            f_right(h, blkidx(-k, xq, 0)).wait_send()
            f_left(h, blkidx(k, xq, 0)).wait_send()

        loop(0, 6, drain_f)

        def drain_long(xq):
            if h == 0:
                f_right(h, blkidx(-3, xq, 0)).wait_send()
            else:
                f_left(h, blkidx(3, xq, 0)).wait_send()
            z_copy(h, h, 4, xq).wait_send()

        loop(0, 2, drain_long)

        def drain_s(e):
            f_sib(h, blkidx(div(e, 2), rem(e, 2), 0)).wait_send()
            sib_copy(h, e).wait_send()

        loop(0, 16, drain_s)

        def drain_z(e):
            z_copy(h, rem(e, 2), 1 + div(e, 4), rem(div(e, 2), 2)).wait_send()

        loop(0, 12, drain_z)
        x_copy(h).wait_send()

        def drain_rep(i):
            rs_copy(h, rem(rep + i, NREP)).wait_send()
            g_copy(h, i).wait_send()

        loop(1, NREP, drain_rep)

    def drain_w(i):
        r = rem(rep + i, NREP)
        dg_copy(r).wait_send()
        w1_copy(r).wait_send()
        w4_copy(i).wait_send()
        w5_copy(i).wait_send()
        w6_copy(i).wait_send()

    loop(1, NREP, drain_w)
    w2_copy.wait_send()
    w3_copy.wait_send()


def place_kernel(a, b, c, out_a, out_b, out_c):
    out_a[...] = a[...]
    out_b[...] = b[...]
    out_c[...] = c[...]


def shards(node_features, weight, cotangent, tile_values, tile_rows, tile_cols, tile_count):
    half, width = TILE, 2 * TILE
    dma = pltpu.SemaphoreType.DMA
    vmem = pltpu.VMEM
    smem_spec = pl.BlockSpec(memory_space=pltpu.SMEM)
    vmem_spec = pl.BlockSpec(memory_space=pltpu.VMEM)
    any_spec = pl.BlockSpec(memory_space=pl.ANY)
    rows = tile_rows[0, 0].T
    outs = pl.pallas_call(
        layer_kernel,
        out_shape=[
            jax.ShapeDtypeStruct((width, width), BF16),
            jax.ShapeDtypeStruct((width, width), BF16),
            jax.ShapeDtypeStruct((width, width), F32),
        ],
        in_specs=[smem_spec] * 3 + [vmem_spec] + [any_spec] * 4,
        out_specs=[vmem_spec] * 3,
        scratch_shapes=[
            vmem((2, NBLK, width, half), BF16),
            vmem((NBLK, SLOT * TILE, width), BF16),
            vmem((NBLK, SLOT, TILE, TILE), jnp.int32),
            vmem((2, POS + 1, TILE, TILE), F32),
            vmem((POS + 1, 8, TILE), F32),
            vmem((8, POS), jnp.int32),
            pltpu.SMEM((8, POS), jnp.int32),
            vmem((width, width), BF16),
            vmem((width, width), BF16),
            vmem((2, NREP, width, half), BF16),
            vmem((2, NREP, width, half), BF16),
            vmem((2, width, half), F32),
            vmem((NREP, 2, 8, TILE), F32),
            vmem((NREP, 2, 8, TILE), F32),
            vmem((width, width), BF16),
            vmem((2, half, width), BF16),
            vmem((2 * NREP, half, TILE), BF16),
            vmem((2 * NREP, half, TILE), BF16),
            vmem((2, 16, half, width), BF16),
            vmem((2, 16, half, width), BF16),
            vmem((2, 16, half, width), BF16),
            vmem((2, 16, half, width), BF16),
            vmem((2, half, width), BF16),
            vmem((2, half, width), BF16),
            vmem((NREP, 32, width), F32),
            vmem((NREP, 32, width), F32),
            vmem((32, width), F32),
            vmem((32, width), F32),
            vmem((32, width), F32),
            vmem((32, width), F32),
            vmem((NZ, 8, TILE), F32),
            vmem((NZ, 8, TILE), F32),
            vmem((8, TILE), F32),
            vmem((NZ, 8, TILE), F32),
            vmem((32, width), F32),
            vmem((NREP, 32, width), F32),
            dma((4,)), dma((NBLK,)), dma,
            dma((2, NBLK)), dma((2, NBLK)), dma((2, NBLK)), dma((2, NBLK)), dma((2,)),
            dma((2, NREP)), dma((2, NREP)), dma((NREP,)), dma((NREP,)), dma((2, NREP)), dma((2, NREP)),
            dma((2, 16)), dma((2, 16)), dma((2, 16)), dma((2, 16)), dma((2,)), dma((2,)),
            dma((NREP,)), dma((NREP,)), dma((2,)), dma((2,)), dma((NZ,)), dma((NZ,)), dma((NZ,)), dma((NZ,)),
            dma((NREP,)), dma((NREP,)),
        ],
        compiler_params=pltpu.CompilerParams(
            collective_id=0, has_side_effects=True, vmem_limit_bytes=56 << 20),
        cost_estimate=pl.CostEstimate(flops=4 << 30, bytes_accessed=9 << 20, transcendentals=1 << 16),
        name="graph_layer",
    )(
        rows, tile_cols[0, 0].T, tile_count.reshape(-1), rows,
        node_features, weight, cotangent, tile_values[0, 0],
    )
    return pl.pallas_call(
        place_kernel,
        out_shape=[jax.ShapeDtypeStruct(out.shape, out.dtype) for out in outs],
        in_specs=[vmem_spec] * 3,
        out_specs=[vmem_spec] * 3,
        name="place",
    )(*outs)


def solution(mesh):
    in_specs = (
        P(("blk", "rep"), None),
        P(),
        P(("blk", "rep"), None),
        P("blk", "rep", None, None, None, None),
        P("blk", "rep", None, None),
        P("blk", "rep", None, None),
        P("blk", "rep", None),
    )
    out_specs = (P(("blk", "rep"), None), P(("blk", "rep"), None), P())
    return jax.shard_map(shards, mesh=mesh, in_specs=in_specs, out_specs=out_specs, check_vma=False)
```

```python
import jax
import jax.numpy as jnp
from jax import lax
from jax.experimental import pallas as pl
from jax.experimental.pallas import tpu as pltpu
from jax.sharding import PartitionSpec as P

TILE = 128
SLOT = 4
MESH = pl.DeviceIdType.MESH
F32 = jnp.float32
BF16 = jnp.bfloat16
NZ, NBLK, NREP, NX = 8, 32, 8, 2
POS = NBLK * SLOT


def rem(a, n):
    return lax.rem(a, jnp.int32(n))


def div(a, n):
    return lax.div(a, jnp.int32(n))


def loop(lo, hi, body):
    lax.fori_loop(lo, hi, lambda i, _: (body(i), 0)[1], 0)


def layer_kernel(
    rows_ref, cols_ref, count_ref, rowsv_ref, x_hbm, w_hbm, ct_hbm, tiles_hbm,
    act_ref, fgrad_ref, wgrad_ref,
    xbuf, dbuf, stage, sbuf, degs, idxv, idxs, wbuf, ctbuf,
    rs_src, rs_dst, own, deg_src, deg_dst, mixed, ngt, gt0, gt1,
    ss, sr, zs, zr, xs, xr,
    wp_src, wp_dst, w2g, w4s, w4r, w5s, w5r, w6s, w6r,
    in_sem, tile_sem, idx_sem,
    x_recv, xr_send, xl_send, xs_send, xx_send,
    rs_send, rs_recv, dg_send, dg_recv, g_send, g_recv,
    ss_send, ss_recv, z_send, z_recv, xf_send, xf_recv,
    w1_send, w1_recv, w2_send, w2_recv, w4_send, w4_recv, w5_send, w5_recv, w6_send, w6_recv,
):
    b = lax.axis_index("blk")
    rep = lax.axis_index("rep")
    z, xh, c = div(b, 4), rem(div(b, 2), 2), rem(b, 2)
    gts = (gt0, gt1)

    def blkidx(dz, xq, cq):
        return rem(z + dz + 8, 8) * 4 + rem(xh + xq, 2) * 2 + rem(c + cq, 2)

    def zdev(dz):
        return (blkidx(dz, 0, 0), rep)

    right, left = zdev(1), zdev(-1)
    sibling = (blkidx(0, 0, 1), rep)
    xmate = (blkidx(0, 1, 0), rep)

    def repdev(i):
        return (b, rem(rep + i, NREP))

    def remote(src, dst, send, recv, dev):
        return pltpu.make_async_remote_copy(
            src_ref=src, dst_ref=dst, send_sem=send, recv_sem=recv, device_id=dev, device_id_type=MESH)

    def own_load(h):
        return pltpu.make_async_copy(x_hbm.at[:, pl.ds(h * TILE, TILE)], xbuf.at[h, b], in_sem.at[h])

    def tile_load(p):
        zi, q = div(p, 4), rem(p, 4)
        return pltpu.make_async_copy(tiles_hbm.at[group_at(zi, q)], stage.at[p], tile_sem.at[p])

    def group_at(zi, q):
        odd = rem(zi, 2)
        dz = div(zi, 2) * (1 - 2 * odd) - odd
        return blkidx(dz, div(q, 2), rem(q, 2))

    w_load = pltpu.make_async_copy(w_hbm, wbuf, in_sem.at[2])
    ct_load = pltpu.make_async_copy(ct_hbm, ctbuf, in_sem.at[3])
    idx_copy = pltpu.make_async_copy(idxv, idxs, idx_sem)
    own_load(0).start()
    own_load(1).start()
    bar = pltpu.get_barrier_semaphore()
    for dev in (sibling, xmate, (blkidx(0, 1, 1), rep)):
        pl.semaphore_signal(bar, inc=1, device_id=dev, device_id_type=MESH)
    loop(1, NZ, lambda i: pl.semaphore_signal(bar, inc=1, device_id=zdev(i), device_id_type=MESH))
    loop(1, NREP, lambda i: pl.semaphore_signal(bar, inc=1, device_id=repdev(i), device_id_type=MESH))

    own_load(0).wait()
    own_load(1).wait()
    pl.semaphore_wait(bar, 17)

    def f_right(h, j):
        return remote(xbuf.at[h, j], xbuf.at[h, j], xr_send.at[h, j], x_recv.at[h, j], right)

    def f_left(h, j):
        return remote(xbuf.at[h, j], xbuf.at[h, j], xl_send.at[h, j], x_recv.at[h, j], left)

    def f_sib(h, j):
        return remote(xbuf.at[h, j], xbuf.at[h, j], xs_send.at[h, j], x_recv.at[h, j], sibling)

    def f_mate(h):
        return remote(xbuf.at[h, b], xbuf.at[h, b], xx_send.at[h], x_recv.at[h, b], xmate)

    def f_wait(h, j):
        f_sib(h, j).wait_recv()

    def start_own(h):
        f_mate(h).start()
        f_right(h, b).start()
        f_left(h, b).start()
        f_sib(h, b).start()

    start_own(0)
    start_own(1)
    loop(0, NBLK, lambda p: tile_load(p).start())
    w_load.start()
    ct_load.start()

    def first_pos(j):
        cj, xj, zj = j & 1, (j >> 1) & 1, j >> 2
        dz = (zj - z + 8) & 7
        zi = jnp.where(dz < 4, 2 * dz, 15 - 2 * dz)
        q = ((xj + xh) & 1) * 2 + ((cj + c) & 1)
        return (zi * 4 + q) * SLOT

    idxv[...] = jnp.zeros((8, TILE), jnp.int32)
    idxv[0:SLOT, 0:NBLK] = rowsv_ref[...]
    group = lax.broadcasted_iota(jnp.int32, (NBLK, TILE), 0)
    lane = lax.broadcasted_iota(jnp.int32, (NBLK, TILE), 1)
    group_pos, lane_pos = first_pos(group), first_pos(lane & (NBLK - 1))
    row_l = [jnp.broadcast_to(idxv[s:s + 1, :], (TILE, TILE)) for s in range(SLOT)]
    row_s = [jnp.transpose(row)[0:NBLK] for row in row_l]
    last = jnp.full((NBLK, TILE), -1, jnp.int32)
    for t in range(SLOT):
        last = jnp.maximum(last, jnp.where(row_s[t] == lane, group_pos + t, -1))
    last = jnp.max(last, axis=0, keepdims=True)
    for s in range(SLOT):
        prev = jnp.full((NBLK, TILE), -1, jnp.int32)
        for t in range(SLOT):
            before = (row_s[t] == row_l[s][0:NBLK]) & (group_pos + t < lane_pos + s)
            prev = jnp.maximum(prev, jnp.where(before, group_pos + t, -1))
        prev = jnp.max(prev, axis=0, keepdims=True)
        idxv[s:s + 1, :] = jnp.where(prev < 0, POS, prev)
    idxv[SLOT:SLOT + 1, :] = jnp.where(last < 0, POS, last)
    idx_copy.start()
    for h in range(2):
        sbuf[h, POS] = jnp.zeros((TILE, TILE), F32)
    degs[POS] = jnp.zeros((8, TILE), F32)


    def prep(p, j):
        tile_load(p).wait()
        for s in range(SLOT):
            live = s < count_ref[j]
            col = cols_ref[s, j]
            m0 = jnp.where(live & (col == 0), 1.0, 0.0).astype(F32)
            m1 = jnp.where(live & (col == 1), 1.0, 0.0).astype(F32)
            tile = stage[p, s].astype(F32)
            dbuf[j, pl.ds(s * TILE, TILE), 0:TILE] = (tile * m0).astype(BF16)
            dbuf[j, pl.ds(s * TILE, TILE), TILE:2 * TILE] = (tile * m1).astype(BF16)
        ones = jnp.ones((16, 2 * TILE), BF16)
        sums = lax.dot_general(ones, dbuf[j], (((1,), (1,)), ((), ())), preferred_element_type=F32)
        for s in range(SLOT):
            degs[p * SLOT + s] = sums[0:8, s * TILE:(s + 1) * TILE] + degs[idxs[s, j]]

    def process(h, p):
        zi, q = div(p, 4), rem(p, 4)
        j = group_at(zi, q)
        pl.when(rem(q, 2) == 1)(lambda: f_wait(h, j))
        if h == 0:
            prep(p, j)
        prod = jnp.dot(dbuf[j], xbuf[h, j], preferred_element_type=F32)
        for s in range(SLOT):
            sbuf[h, p * SLOT + s] = prod[s * TILE:(s + 1) * TILE] + sbuf[h, idxs[s, j]]

    def rs_copy(h, r):
        return remote(rs_src.at[h, r], rs_dst.at[h, rep], rs_send.at[h, r], rs_recv.at[h, rep], (b, r))

    def rs_arrival(h, r):
        return remote(rs_src.at[h, r], rs_dst.at[h, r], rs_send.at[h, r], rs_recv.at[h, r], (b, r))

    def dg_copy(r):
        return remote(deg_src.at[r], deg_dst.at[rep], dg_send.at[r], dg_recv.at[rep], (b, r))

    def dg_arrival(r):
        return remote(deg_src.at[r], deg_dst.at[r], dg_send.at[r], dg_recv.at[r], (b, r))

    def forward_open(h):
        jx = blkidx(0, 1, 0)
        f_wait(h, jx)
        f_right(h, jx).start()
        f_left(h, jx).start()
        f_sib(h, jx).start()

    def forward_step(h, k):
        far_r, far_l = 4 - h, 3 + h

        def event(v):
            sgn, xq = rem(v, 2), div(v, 2)
            j = blkidx(k * (2 * sgn - 1), xq, 0)
            f_wait(h, j)
            if k < far_r:
                pl.when(sgn == 0)(lambda: f_right(h, j).start())
            if k < far_l:
                pl.when(sgn == 1)(lambda: f_left(h, j).start())
            f_sib(h, j).start()
            n = 1 if k == 1 else 2
            p0 = v if k == 1 else 4 + (k - 2) * 8 + v * 2
            loop(p0, p0 + n, lambda p: process(h, p))

        loop(0, 4, event)

    def forward_close(h):
        def far(xq):
            j = blkidx(4, xq, 0)
            loop(20 + xq * 4, 24 + xq * 4, lambda p: process(h, p))
            f_wait(h, j)
            f_sib(h, j).start()

        loop(0, 2, far)
        loop(28, 32, lambda p: process(h, p))

    def send_sums(h):
        def chunk(i):
            r = rem(rep + i, NREP)
            for t in range(2):
                rs_src[h, r, pl.ds(t * TILE, TILE)] = sbuf[h, idxs[SLOT, 2 * r + t]].astype(BF16)
            rs_copy(h, r).start()
            if h == 0:
                for t in range(2):
                    deg_src[r, t] = degs[idxs[SLOT, 2 * r + t]]
                dg_copy(r).start()

        loop(1, NREP, chunk)
        for t in range(2):
            own[h, pl.ds(t * TILE, TILE)] = sbuf[h, idxs[SLOT, 2 * rep + t]]
            if h == 0:
                deg_src[rep, t] = degs[idxs[SLOT, 2 * rep + t]]

    forward_open(0)
    forward_open(1)
    idx_copy.wait()
    for k in range(1, 4):
        forward_step(0, k)
        if k > 1:
            forward_step(1, k - 1)
    forward_close(0)
    send_sums(0)
    forward_step(1, 3)
    forward_close(1)
    send_sums(1)

    w_load.wait()
    ct_load.wait()
    loop(1, NREP, lambda i: dg_arrival(rem(rep + i, NREP)).wait_recv())
    deg = deg_src[rep]
    for i in range(1, NREP):
        deg = deg + deg_dst[rem(rep + i, NREP)]
    scale = lax.rsqrt(deg + 1.0)
    scale_row = jnp.concatenate([scale[0, 0:1], scale[1, 0:1]], axis=1)
    scale_col = [jnp.transpose(jnp.broadcast_to(scale[t, 0:1], (TILE, TILE))) for t in range(2)]
    for h in range(2):
        def add(i):
            r = rem(rep + i, NREP)
            rs_arrival(h, r).wait_recv()
            own[h] += rs_dst[h, r].astype(F32)

        loop(1, NREP, add)
        for t in range(2):
            part = own[h, pl.ds(t * TILE, TILE)] + xbuf[h, b, pl.ds(t * TILE, TILE)].astype(F32)
            mixed[pl.ds(t * TILE, TILE), h * TILE:(h + 1) * TILE] = (part * scale_col[t]).astype(BF16)
    pre = jnp.dot(mixed[...], wbuf[...], preferred_element_type=F32)
    sig = 1.0 / (1.0 + jnp.exp(-pre))
    act_ref[...] = (pre * sig).astype(BF16)
    act_grad = (ctbuf[...].astype(F32) * sig * (1.0 + pre * (1.0 - sig))).astype(BF16)

    def g_copy(h, i):
        mine = gts[h].at[pl.ds(2 * rep, 2)]
        return remote(mine, mine, g_send.at[h, i], g_recv.at[h, rep], repdev(i))

    def g_arrival(h, r):
        part = gts[h].at[pl.ds(2 * r, 2)]
        return remote(part, part, g_send.at[h, 0], g_recv.at[h, r], (b, r))

    for h in range(2):
        back = lax.dot_general(
            wbuf[h * TILE:(h + 1) * TILE, :], act_grad, (((1,), (1,)), ((), ())), preferred_element_type=F32)
        grad = (back * scale_row).astype(BF16)
        ngt[h] = grad
        for t in range(2):
            gts[h][2 * rep + t] = grad[:, t * TILE:(t + 1) * TILE]
        loop(1, NREP, lambda i: g_copy(h, i).start())

    def w1_copy(r):
        return remote(wp_src.at[r], wp_dst.at[rep], w1_send.at[r], w1_recv.at[rep], (b, r))

    def w1_arrival(r):
        return remote(wp_src.at[r], wp_dst.at[r], w1_send.at[r], w1_recv.at[r], (b, r))

    quad = xh * 2 + c
    others = ((0, 1), (1, 0), (1, 1))

    def w2_copy(xq, cq):
        return remote(w2g.at[quad], w2g.at[quad], w2_send.at[xq * 2 + cq], w2_recv.at[quad], (blkidx(0, xq, cq), rep))

    def w2_arrival(xq, cq):
        i = rem(xh + xq, 2) * 2 + rem(c + cq, 2)
        return remote(w2g.at[i], w2g.at[i], w2_send.at[0], w2_recv.at[i], sibling)

    def w4_copy(i):
        zz = rem(z + i, NZ)
        return remote(w4s.at[zz], w4r.at[z], w4_send.at[zz], w4_recv.at[z], zdev(i))

    def w4_arrival(zz):
        return remote(w4s.at[zz], w4r.at[zz], w4_send.at[zz], w4_recv.at[zz], right)

    def w5_copy(i):
        return remote(w5s, w5r.at[z], w5_send.at[i], w5_recv.at[z], zdev(i))

    def w5_arrival(zz):
        return remote(w5s, w5r.at[zz], w5_send.at[0], w5_recv.at[zz], right)

    def w6_copy(i):
        return remote(w6s, w6r.at[rep], w6_send.at[i], w6_recv.at[rep], repdev(i))

    def w6_arrival(r):
        return remote(w6s, w6r.at[r], w6_send.at[0], w6_recv.at[r], (b, r))

    part = lax.dot_general(mixed[...], act_grad, (((0,), (0,)), ((), ())), preferred_element_type=F32)
    for r in range(NREP):
        wp_src[r] = part[r * 32:(r + 1) * 32].astype(BF16)

    def w_step2():
        loop(1, NREP, lambda i: w1_arrival(rem(rep + i, NREP)).wait_recv())
        wp_dst[rep] = wp_src[rep]
        w2g[quad] = sum(wp_dst[r].astype(F32) for r in range(NREP))
        for xq, cq in others:
            w2_copy(xq, cq).start()

    def w_step4():
        for xq, cq in others:
            w2_arrival(xq, cq).wait_recv()
        both = (w2g[0] + w2g[1]) + (w2g[2] + w2g[3])
        for k in range(NZ):
            w4s[k] = both[(k // 2) * 8:(k // 2) * 8 + 8, (k % 2) * TILE:(k % 2) * TILE + TILE]
        loop(1, NZ, lambda i: w4_copy(i).start())

    def w_step5():
        loop(1, NZ, lambda i: w4_arrival(rem(z + i, NZ)).wait_recv())
        w4r[z] = w4s[z]
        w5s[...] = sum(w4r[k] for k in range(NZ))
        loop(1, NZ, lambda i: w5_copy(i).start())

    def w_step6():
        loop(1, NZ, lambda i: w5_arrival(rem(z + i, NZ)).wait_recv())
        w5r[z] = w5s[...]
        for k in range(NZ):
            w6s[(k // 2) * 8:(k // 2) * 8 + 8, (k % 2) * TILE:(k % 2) * TILE + TILE] = w5r[k]
        loop(1, NREP, lambda i: w6_copy(i).start())

    def w_step7():
        loop(1, NREP, lambda i: w6_arrival(rem(rep + i, NREP)).wait_recv())
        w6r[rep] = w6s[...]
        for r in range(NREP):
            wgrad_ref[r * 32:(r + 1) * 32] = w6r[r] * (NBLK * NREP * 2 * TILE) ** -0.5

    def out_t(h, j):
        left_side = jnp.concatenate([gts[h][rows_ref[s, j]] for s in range(SLOT)], axis=1)
        return jnp.dot(left_side, dbuf[j], preferred_element_type=F32)

    def sib_copy(h, k):
        return remote(ss.at[h, k], sr.at[h, k], ss_send.at[h, k], ss_recv.at[h, k], sibling)

    def z_copy(h, d, m, xq):
        i = (d * 4 + m - 1) * 2 + xq
        dev = (jnp.where(d == 0, right[0], left[0]), rep)
        return remote(zs.at[h, i], zr.at[h, i], z_send.at[h, i], z_recv.at[h, i], dev)

    def z_arrival(h, d, m, xq):
        i = (d * 4 + m) * 2 + xq
        return remote(zs.at[h, i], zr.at[h, i], z_send.at[h, i], z_recv.at[h, i], right)

    def z_value(h, d, m, xq):
        return zr[h, (d * 4 + m) * 2 + xq].astype(F32)

    def x_copy(h, k):
        return remote(xs.at[h, k], xr.at[h, k], xf_send.at[h, k], xf_recv.at[h, k], xmate)

    def sib_term(h, d, m, xq):
        dz = m * (1 - 2 * d)
        k = rem(dz + 8, 8) * 2 + xq
        ss[h, k] = out_t(h, blkidx(dz, xq, 1)).astype(BF16)
        sib_copy(h, k).start()

    def own_term(h, d, m, xq):
        dz = m * (1 - 2 * d)
        zrel = rem(dz + 8, 8)
        k = zrel * 2 + xq
        value = out_t(h, blkidx(dz, xq, 0))
        sib_copy(h, k).wait_recv()
        value = value + sr[h, k].astype(F32)
        if h == 1 and xq == 0:
            x_copy(h, zrel).wait_recv()
            value = value + xr[h, zrel].astype(F32)
        return value

    def cross_term(d, m):
        zrel = rem(m * (1 - 2 * d) + 8, 8)
        xs[1, zrel] = own_term(1, d, m, 1).astype(BF16)
        x_copy(1, zrel).start()

    def start_on(h, d, m, xq):
        zs[h, (d * 4 + m - 1) * 2 + xq] = own_term(h, d, m, xq).astype(BF16)
        z_copy(h, d, m, xq).start()

    def pass_on(h, d, m, xq):
        value = own_term(h, d, m, xq)
        i = (d * 4 + m) * 2 + xq
        z_arrival(h, d, m, xq).wait_recv()
        zs[h, i - 2] = (value + zr[h, i].astype(F32)).astype(BF16)
        z_copy(h, d, m, xq).start()

    def arrive(h):
        loop(1, NREP, lambda i: g_arrival(h, rem(rep + i, NREP)).wait_recv())

    def open_0():
        arrive(0)
        loop(1, NREP, lambda i: w1_copy(rem(rep + i, NREP)).start())
        loop(0, 2, lambda q: sib_term(0, 0, 4, q))
        loop(0, 2, lambda q: sib_term(0, 1, 3, q))
        loop(0, 2, lambda q: start_on(0, 0, 4, q))
        loop(0, 2, lambda q: sib_term(0, 0, 3, q))
        loop(0, 2, lambda q: start_on(0, 1, 3, q))

    def open_1():
        arrive(1)
        loop(0, 2, lambda q: sib_term(1, 1, 4, 1 - q))
        loop(0, 4, lambda e: sib_term(1, rem(e, 2), 3, 1 - div(e, 2)))
        cross_term(1, 4)
        loop(0, 2, lambda d: cross_term(d, 3))
        loop(0, 4, lambda e: sib_term(1, rem(e, 2), 2, 1 - div(e, 2)))

    def third_0():
        def body(q):
            sib_term(0, 0, 2, q)
            sib_term(0, 1, 2, q)
            pass_on(0, 0, 3, q)

        loop(0, 2, body)

    def second_0():
        def body(e):
            d, q = rem(e, 2), div(e, 2)
            sib_term(0, d, 1, q)
            pass_on(0, d, 2, q)

        loop(0, 4, body)

    def first_0():
        loop(0, 2, lambda q: sib_term(0, 0, 0, q))
        loop(0, 4, lambda e: pass_on(0, rem(e, 2), 1, div(e, 2)))

    def third_1():
        loop(0, 2, lambda d: cross_term(d, 2))
        loop(0, 4, lambda e: sib_term(1, rem(e, 2), 1, 1 - div(e, 2)))
        start_on(1, 1, 4, 0)
        start_on(1, 0, 3, 0)

    def second_1():
        loop(0, 2, lambda d: cross_term(d, 1))
        loop(0, 2, lambda q: sib_term(1, 0, 0, 1 - q))
        pass_on(1, 1, 3, 0)

    def first_1():
        cross_term(0, 0)
        loop(0, 2, lambda d: pass_on(1, d, 2, 0))

    def last_1():
        loop(0, 2, lambda d: pass_on(1, d, 1, 0))

    def settled(h, xq):
        value = own_term(h, 0, 0, xq)
        z_arrival(h, 0, 0, xq).wait_recv()
        z_arrival(h, 1, 0, xq).wait_recv()
        return value + z_value(h, 0, 0, xq) + z_value(h, 1, 0, xq)

    def to_mate():
        xs[0, 0] = settled(0, 1).astype(BF16)
        x_copy(0, 0).start()

    def finish(h):
        value = settled(h, 0) + ngt[h].astype(F32)
        if h == 0:
            x_copy(0, 0).wait_recv()
            value = value + xr[0, 0].astype(F32)
        fgrad_ref[:, h * TILE:(h + 1) * TILE] = jnp.transpose(value).astype(BF16)

    def drain_forward(h):
        f_mate(h).wait_send()

        def near(e):
            k, xq = div(e, 2), rem(e, 2)
            f_right(h, blkidx(-k, xq, 0)).wait_send()
            f_left(h, blkidx(k, xq, 0)).wait_send()

        def farthest(xq):
            if h == 0:
                f_right(h, blkidx(-3, xq, 0)).wait_send()
            else:
                f_left(h, blkidx(3, xq, 0)).wait_send()

        loop(0, 6, near)
        loop(0, 2, farthest)
        loop(0, 16, lambda e: f_sib(h, blkidx(div(e, 2), rem(e, 2), 0)).wait_send())
        loop(1, NREP, lambda i: rs_copy(h, rem(rep + i, NREP)).wait_send())

    def drain_backward(h):
        cols = 2 - h

        def near(e):
            z_copy(h, rem(e, 2), 1 + div(e, 2 * cols), rem(div(e, 2), cols)).wait_send()

        loop(0, 6 * cols, near)
        loop(0, cols, lambda xq: z_copy(h, h, 4, xq).wait_send())
        loop(0, NZ if h else 1, lambda k: x_copy(h, k).wait_send())
        loop(0, 16, lambda e: sib_copy(h, e).wait_send())
        loop(1, NREP, lambda i: g_copy(h, i).wait_send())

    def drain_weight(i):
        r = rem(rep + i, NREP)
        dg_copy(r).wait_send()
        w1_copy(r).wait_send()
        w4_copy(i).wait_send()
        w5_copy(i).wait_send()
        w6_copy(i).wait_send()

    drain_forward(0)
    drain_forward(1)
    open_0()
    open_1()
    third_0()
    w_step2()
    third_1()
    second_0()
    w_step4()
    second_1()
    first_0()
    w_step5()
    first_1()
    to_mate()
    w_step6()
    last_1()
    drain_backward(0)
    drain_backward(1)
    finish(0)
    w_step7()
    finish(1)
    loop(1, NREP, drain_weight)
    for xq, cq in others:
        w2_copy(xq, cq).wait_send()


def place_kernel(a, b, c, out_a, out_b, out_c):
    out_a[...] = a[...]
    out_b[...] = b[...]
    out_c[...] = c[...]


def shards(node_features, weight, cotangent, tile_values, tile_rows, tile_cols, tile_count):
    half, width = TILE, 2 * TILE
    dma = pltpu.SemaphoreType.DMA
    vmem = pltpu.VMEM
    smem_spec = pl.BlockSpec(memory_space=pltpu.SMEM)
    vmem_spec = pl.BlockSpec(memory_space=pltpu.VMEM)
    any_spec = pl.BlockSpec(memory_space=pl.ANY)
    rows = tile_rows[0, 0].T
    outs = pl.pallas_call(
        layer_kernel,
        out_shape=[
            jax.ShapeDtypeStruct((width, width), BF16),
            jax.ShapeDtypeStruct((width, width), BF16),
            jax.ShapeDtypeStruct((width, width), F32),
        ],
        in_specs=[smem_spec] * 3 + [vmem_spec] + [any_spec] * 4,
        out_specs=[vmem_spec] * 3,
        scratch_shapes=[
            vmem((2, NBLK, width, half), BF16),
            vmem((NBLK, SLOT * TILE, width), BF16),
            vmem((NBLK, SLOT, TILE, TILE), jnp.int32),
            vmem((2, POS + 1, TILE, TILE), F32),
            vmem((POS + 1, 8, TILE), F32),
            vmem((8, POS), jnp.int32),
            pltpu.SMEM((8, POS), jnp.int32),
            vmem((width, width), BF16),
            vmem((width, width), BF16),
            vmem((2, NREP, width, half), BF16),
            vmem((2, NREP, width, half), BF16),
            vmem((2, width, half), F32),
            vmem((NREP, 2, 8, TILE), F32),
            vmem((NREP, 2, 8, TILE), F32),
            vmem((width, width), BF16),
            vmem((2, half, width), BF16),
            vmem((2 * NREP, half, TILE), BF16),
            vmem((2 * NREP, half, TILE), BF16),
            vmem((2, 16, half, width), BF16),
            vmem((2, 16, half, width), BF16),
            vmem((2, 16, half, width), BF16),
            vmem((2, 16, half, width), BF16),
            vmem((2, NZ, half, width), BF16),
            vmem((2, NZ, half, width), BF16),
            vmem((NREP, 32, width), BF16),
            vmem((NREP, 32, width), BF16),
            vmem((4, 32, width), F32),
            vmem((NZ, 8, TILE), F32),
            vmem((NZ, 8, TILE), F32),
            vmem((8, TILE), F32),
            vmem((NZ, 8, TILE), F32),
            vmem((32, width), F32),
            vmem((NREP, 32, width), F32),
            dma((4,)), dma((NBLK,)), dma,
            dma((2, NBLK)), dma((2, NBLK)), dma((2, NBLK)), dma((2, NBLK)), dma((2,)),
            dma((2, NREP)), dma((2, NREP)), dma((NREP,)), dma((NREP,)), dma((2, NREP)), dma((2, NREP)),
            dma((2, 16)), dma((2, 16)), dma((2, 16)), dma((2, 16)), dma((2, NZ)), dma((2, NZ)),
            dma((NREP,)), dma((NREP,)), dma((4,)), dma((4,)), dma((NZ,)), dma((NZ,)), dma((NZ,)), dma((NZ,)),
            dma((NREP,)), dma((NREP,)),
        ],
        compiler_params=pltpu.CompilerParams(
            collective_id=0, has_side_effects=True, vmem_limit_bytes=56 << 20),
        cost_estimate=pl.CostEstimate(flops=4 << 30, bytes_accessed=9 << 20, transcendentals=1 << 16),
        name="graph_layer",
    )(
        rows, tile_cols[0, 0].T, tile_count.reshape(-1), rows,
        node_features, weight, cotangent, tile_values[0, 0],
    )
    return pl.pallas_call(
        place_kernel,
        out_shape=[jax.ShapeDtypeStruct(out.shape, out.dtype) for out in outs],
        in_specs=[vmem_spec] * 3,
        out_specs=[vmem_spec] * 3,
        name="place",
    )(*outs)


def solution(mesh):
    in_specs = (
        P(("blk", "rep"), None),
        P(),
        P(("blk", "rep"), None),
        P("blk", "rep", None, None, None, None),
        P("blk", "rep", None, None),
        P("blk", "rep", None, None),
        P("blk", "rep", None),
    )
    out_specs = (P(("blk", "rep"), None), P(("blk", "rep"), None), P())
    return jax.shard_map(shards, mesh=mesh, in_specs=in_specs, out_specs=out_specs, check_vma=False)
```

```python
import jax
import jax.numpy as jnp
from jax import lax
from jax.experimental import pallas as pl
from jax.experimental.pallas import tpu as pltpu
from jax.sharding import PartitionSpec as P

TILE = 128
SLOT = 4
MESH = pl.DeviceIdType.MESH
F32 = jnp.float32
BF16 = jnp.bfloat16
NZ, NBLK, NREP, NX = 8, 32, 8, 2
POS = NBLK * SLOT


def rem(a, n):
    return lax.rem(a, jnp.int32(n))


def div(a, n):
    return lax.div(a, jnp.int32(n))


def loop(lo, hi, body):
    lax.fori_loop(lo, hi, lambda i, _: (body(i), 0)[1], 0)


def layer_kernel(
    rows_ref, cols_ref, count_ref, rowsv_ref, x_hbm, w_hbm, ct_hbm, tiles_hbm,
    act_ref, fgrad_ref, wgrad_ref,
    xbuf, dbuf, stage, sbuf, degs, idxv, idxs, wbuf, ctbuf,
    rs_src, rs_dst, own, deg_src, deg_dst, mixed, ngt, gt0, gt1,
    ss, sr, zs, zr, xs, xr,
    wp_src, wp_dst, w2g, w4s, w4r, w5s, w5r, w6s, w6r,
    in_sem, tile_sem, idx_sem,
    x_recv, xr_send, xl_send, xs_send, xx_send,
    rs_send, rs_recv, dg_send, dg_recv, g_send, g_recv,
    ss_send, ss_recv, z_send, z_recv, xf_send, xf_recv,
    w1_send, w1_recv, w2_send, w2_recv, w4_send, w4_recv, w5_send, w5_recv, w6_send, w6_recv,
):
    b = lax.axis_index("blk")
    rep = lax.axis_index("rep")
    z, xh, c = div(b, 4), rem(div(b, 2), 2), rem(b, 2)
    gts = (gt0, gt1)

    def blkidx(dz, xq, cq):
        return rem(z + dz + 8, 8) * 4 + rem(xh + xq, 2) * 2 + rem(c + cq, 2)

    def zdev(dz):
        return (blkidx(dz, 0, 0), rep)

    right, left = zdev(1), zdev(-1)
    sibling = (blkidx(0, 0, 1), rep)
    xmate = (blkidx(0, 1, 0), rep)

    def repdev(i):
        return (b, rem(rep + i, NREP))

    def remote(src, dst, send, recv, dev):
        return pltpu.make_async_remote_copy(
            src_ref=src, dst_ref=dst, send_sem=send, recv_sem=recv, device_id=dev, device_id_type=MESH)

    def own_load(h):
        return pltpu.make_async_copy(x_hbm.at[:, pl.ds(h * TILE, TILE)], xbuf.at[h, b], in_sem.at[h])

    def tile_load(p):
        zi, q = div(p, 4), rem(p, 4)
        return pltpu.make_async_copy(tiles_hbm.at[group_at(zi, q)], stage.at[p], tile_sem.at[p])

    def group_at(zi, q):
        odd = rem(zi, 2)
        dz = div(zi, 2) * (1 - 2 * odd) - odd
        return blkidx(dz, div(q, 2), rem(q, 2))

    w_load = pltpu.make_async_copy(w_hbm, wbuf, in_sem.at[2])
    ct_load = pltpu.make_async_copy(ct_hbm, ctbuf, in_sem.at[3])
    idx_copy = pltpu.make_async_copy(idxv, idxs, idx_sem)
    own_load(0).start()
    own_load(1).start()
    bar = pltpu.get_barrier_semaphore()
    for dev in (sibling, xmate, (blkidx(0, 1, 1), rep)):
        pl.semaphore_signal(bar, inc=1, device_id=dev, device_id_type=MESH)
    loop(1, NZ, lambda i: pl.semaphore_signal(bar, inc=1, device_id=zdev(i), device_id_type=MESH))
    loop(1, NREP, lambda i: pl.semaphore_signal(bar, inc=1, device_id=repdev(i), device_id_type=MESH))

    own_load(0).wait()
    own_load(1).wait()
    pl.semaphore_wait(bar, 17)

    def f_right(h, j):
        return remote(xbuf.at[h, j], xbuf.at[h, j], xr_send.at[h, j], x_recv.at[h, j], right)

    def f_left(h, j):
        return remote(xbuf.at[h, j], xbuf.at[h, j], xl_send.at[h, j], x_recv.at[h, j], left)

    def f_sib(h, j):
        return remote(xbuf.at[h, j], xbuf.at[h, j], xs_send.at[h, j], x_recv.at[h, j], sibling)

    def f_mate(h):
        return remote(xbuf.at[h, b], xbuf.at[h, b], xx_send.at[h], x_recv.at[h, b], xmate)

    def f_wait(h, j):
        f_sib(h, j).wait_recv()

    def start_own(h):
        f_right(h, b).start()
        f_left(h, b).start()
        f_sib(h, b).start()

    f_mate(0).start()
    f_mate(1).start()
    start_own(0)
    start_own(1)
    loop(0, NBLK, lambda p: tile_load(p).start())
    w_load.start()
    ct_load.start()

    def first_pos(j):
        cj, xj, zj = j & 1, (j >> 1) & 1, j >> 2
        dz = (zj - z + 8) & 7
        zi = jnp.where(dz < 4, 2 * dz, 15 - 2 * dz)
        q = ((xj + xh) & 1) * 2 + ((cj + c) & 1)
        return (zi * 4 + q) * SLOT

    idxv[...] = jnp.zeros((8, TILE), jnp.int32)
    idxv[0:SLOT, 0:NBLK] = rowsv_ref[...]
    group = lax.broadcasted_iota(jnp.int32, (NBLK, TILE), 0)
    lane = lax.broadcasted_iota(jnp.int32, (NBLK, TILE), 1)
    group_pos, lane_pos = first_pos(group), first_pos(lane & (NBLK - 1))
    row_l = [jnp.broadcast_to(idxv[s:s + 1, :], (TILE, TILE)) for s in range(SLOT)]
    row_s = [jnp.transpose(row)[0:NBLK] for row in row_l]
    last = jnp.full((NBLK, TILE), -1, jnp.int32)
    for t in range(SLOT):
        last = jnp.maximum(last, jnp.where(row_s[t] == lane, group_pos + t, -1))
    last = jnp.max(last, axis=0, keepdims=True)
    for s in range(SLOT):
        prev = jnp.full((NBLK, TILE), -1, jnp.int32)
        for t in range(SLOT):
            before = (row_s[t] == row_l[s][0:NBLK]) & (group_pos + t < lane_pos + s)
            prev = jnp.maximum(prev, jnp.where(before, group_pos + t, -1))
        prev = jnp.max(prev, axis=0, keepdims=True)
        idxv[s:s + 1, :] = jnp.where(prev < 0, POS, prev)
    idxv[SLOT:SLOT + 1, :] = jnp.where(last < 0, POS, last)
    idx_copy.start()
    for h in range(2):
        sbuf[h, POS] = jnp.zeros((TILE, TILE), F32)
    degs[POS] = jnp.zeros((8, TILE), F32)


    def prep(p, j):
        tile_load(p).wait()
        for s in range(SLOT):
            live = s < count_ref[j]
            col = cols_ref[s, j]
            m0 = jnp.where(live & (col == 0), 1.0, 0.0).astype(F32)
            m1 = jnp.where(live & (col == 1), 1.0, 0.0).astype(F32)
            tile = stage[p, s].astype(F32)
            dbuf[j, pl.ds(s * TILE, TILE), 0:TILE] = (tile * m0).astype(BF16)
            dbuf[j, pl.ds(s * TILE, TILE), TILE:2 * TILE] = (tile * m1).astype(BF16)
        ones = jnp.ones((16, 2 * TILE), BF16)
        sums = lax.dot_general(ones, dbuf[j], (((1,), (1,)), ((), ())), preferred_element_type=F32)
        for s in range(SLOT):
            degs[p * SLOT + s] = sums[0:8, s * TILE:(s + 1) * TILE] + degs[idxs[s, j]]

    def process(h, p):
        zi, q = div(p, 4), rem(p, 4)
        j = group_at(zi, q)
        pl.when(rem(q, 2) == 1)(lambda: f_wait(h, j))
        if h == 0:
            prep(p, j)
        prod = jnp.dot(dbuf[j], xbuf[h, j], preferred_element_type=F32)
        for s in range(SLOT):
            sbuf[h, p * SLOT + s] = prod[s * TILE:(s + 1) * TILE] + sbuf[h, idxs[s, j]]

    def rs_copy(h, r):
        return remote(rs_src.at[h, r], rs_dst.at[h, rep], rs_send.at[h, r], rs_recv.at[h, rep], (b, r))

    def rs_arrival(h, r):
        return remote(rs_src.at[h, r], rs_dst.at[h, r], rs_send.at[h, r], rs_recv.at[h, r], (b, r))

    def dg_copy(r):
        return remote(deg_src.at[r], deg_dst.at[rep], dg_send.at[r], dg_recv.at[rep], (b, r))

    def dg_arrival(r):
        return remote(deg_src.at[r], deg_dst.at[r], dg_send.at[r], dg_recv.at[r], (b, r))

    def forward_open(h):
        jx = blkidx(0, 1, 0)
        f_wait(h, jx)
        f_right(h, jx).start()
        f_left(h, jx).start()
        f_sib(h, jx).start()

    def forward_step(h, k):
        far_r, far_l = 4 - h, 3 + h

        def event(v):
            sgn, xq = rem(v, 2), div(v, 2)
            j = blkidx(k * (2 * sgn - 1), xq, 0)
            f_wait(h, j)
            if k < far_r:
                pl.when(sgn == 0)(lambda: f_right(h, j).start())
            if k < far_l:
                pl.when(sgn == 1)(lambda: f_left(h, j).start())
            f_sib(h, j).start()
            n = 1 if k == 1 else 2
            p0 = v if k == 1 else 4 + (k - 2) * 8 + v * 2
            loop(p0, p0 + n, lambda p: process(h, p))

        loop(0, 4, event)

    def forward_close(h):
        def far(xq):
            j = blkidx(4, xq, 0)
            f_wait(h, j)
            f_sib(h, j).start()
            loop(20 + xq * 4, 24 + xq * 4, lambda p: process(h, p))

        loop(0, 2, far)
        loop(28, 32, lambda p: process(h, p))

    def send_sums(h):
        def chunk(i):
            r = rem(rep + i, NREP)
            for t in range(2):
                rs_src[h, r, pl.ds(t * TILE, TILE)] = sbuf[h, idxs[SLOT, 2 * r + t]].astype(BF16)
            rs_copy(h, r).start()
            if h == 0:
                for t in range(2):
                    deg_src[r, t] = degs[idxs[SLOT, 2 * r + t]]
                dg_copy(r).start()

        loop(1, NREP, chunk)
        for t in range(2):
            own[h, pl.ds(t * TILE, TILE)] = sbuf[h, idxs[SLOT, 2 * rep + t]]
            if h == 0:
                deg_src[rep, t] = degs[idxs[SLOT, 2 * rep + t]]

    forward_open(0)
    forward_open(1)
    idx_copy.wait()
    for k in range(1, 4):
        forward_step(0, k)
        if k > 1:
            forward_step(1, k - 1)
    forward_close(0)
    send_sums(0)
    forward_step(1, 3)
    forward_close(1)
    send_sums(1)

    w_load.wait()
    ct_load.wait()
    loop(1, NREP, lambda i: dg_arrival(rem(rep + i, NREP)).wait_recv())
    deg = deg_src[rep]
    for i in range(1, NREP):
        deg = deg + deg_dst[rem(rep + i, NREP)]
    scale = lax.rsqrt(deg + 1.0)
    scale_row = jnp.concatenate([scale[0, 0:1], scale[1, 0:1]], axis=1)
    scale_col = [jnp.transpose(jnp.broadcast_to(scale[t, 0:1], (TILE, TILE))) for t in range(2)]
    for h in range(2):
        def add(i):
            r = rem(rep + i, NREP)
            rs_arrival(h, r).wait_recv()
            own[h] += rs_dst[h, r].astype(F32)

        loop(1, NREP, add)
        for t in range(2):
            part = own[h, pl.ds(t * TILE, TILE)] + xbuf[h, b, pl.ds(t * TILE, TILE)].astype(F32)
            mixed[pl.ds(t * TILE, TILE), h * TILE:(h + 1) * TILE] = (part * scale_col[t]).astype(BF16)
    pre = jnp.dot(mixed[...], wbuf[...], preferred_element_type=F32)
    sig = 1.0 / (1.0 + jnp.exp(-pre))
    act_grad = (ctbuf[...].astype(F32) * sig * (1.0 + pre * (1.0 - sig))).astype(BF16)

    def g_copy(h, i):
        mine = gts[h].at[pl.ds(2 * rep, 2)]
        return remote(mine, mine, g_send.at[h, i], g_recv.at[h, rep], repdev(i))

    def g_arrival(h, r):
        part = gts[h].at[pl.ds(2 * r, 2)]
        return remote(part, part, g_send.at[h, 0], g_recv.at[h, r], (b, r))

    for h in range(2):
        back = lax.dot_general(
            wbuf[h * TILE:(h + 1) * TILE, :], act_grad, (((1,), (1,)), ((), ())), preferred_element_type=F32)
        grad = (back * scale_row).astype(BF16)
        ngt[h] = grad
        for t in range(2):
            gts[h][2 * rep + t] = grad[:, t * TILE:(t + 1) * TILE]
        loop(1, NREP, lambda i: g_copy(h, i).start())

    def w1_copy(r):
        return remote(wp_src.at[r], wp_dst.at[rep], w1_send.at[r], w1_recv.at[rep], (b, r))

    def w1_arrival(r):
        return remote(wp_src.at[r], wp_dst.at[r], w1_send.at[r], w1_recv.at[r], (b, r))

    quad = xh * 2 + c
    others = ((0, 1), (1, 0), (1, 1))

    def w2_copy(xq, cq):
        return remote(w2g.at[quad], w2g.at[quad], w2_send.at[xq * 2 + cq], w2_recv.at[quad], (blkidx(0, xq, cq), rep))

    def w2_arrival(xq, cq):
        i = rem(xh + xq, 2) * 2 + rem(c + cq, 2)
        return remote(w2g.at[i], w2g.at[i], w2_send.at[0], w2_recv.at[i], sibling)

    def w4_copy(i):
        zz = rem(z + i, NZ)
        return remote(w4s.at[zz], w4r.at[z], w4_send.at[zz], w4_recv.at[z], zdev(i))

    def w4_arrival(zz):
        return remote(w4s.at[zz], w4r.at[zz], w4_send.at[zz], w4_recv.at[zz], right)

    def w5_copy(i):
        return remote(w5s, w5r.at[z], w5_send.at[i], w5_recv.at[z], zdev(i))

    def w5_arrival(zz):
        return remote(w5s, w5r.at[zz], w5_send.at[0], w5_recv.at[zz], right)

    def w6_copy(i):
        return remote(w6s, w6r.at[rep], w6_send.at[i], w6_recv.at[rep], repdev(i))

    def w6_arrival(r):
        return remote(w6s, w6r.at[r], w6_send.at[0], w6_recv.at[r], (b, r))

    act_ref[...] = (pre * sig).astype(BF16)
    part = lax.dot_general(mixed[...], act_grad, (((0,), (0,)), ((), ())), preferred_element_type=F32)
    for r in range(NREP):
        wp_src[r] = part[r * 32:(r + 1) * 32].astype(BF16)

    def w_step2():
        loop(1, NREP, lambda i: w1_arrival(rem(rep + i, NREP)).wait_recv())
        wp_dst[rep] = wp_src[rep]
        w2g[quad] = sum(wp_dst[r].astype(F32) for r in range(NREP))
        for xq, cq in others:
            w2_copy(xq, cq).start()

    def w_step4():
        for xq, cq in others:
            w2_arrival(xq, cq).wait_recv()
        both = (w2g[0] + w2g[1]) + (w2g[2] + w2g[3])
        for k in range(NZ):
            w4s[k] = both[(k // 2) * 8:(k // 2) * 8 + 8, (k % 2) * TILE:(k % 2) * TILE + TILE]
        loop(1, NZ, lambda i: w4_copy(i).start())

    def w_step5():
        loop(1, NZ, lambda i: w4_arrival(rem(z + i, NZ)).wait_recv())
        w4r[z] = w4s[z]
        w5s[...] = sum(w4r[k] for k in range(NZ))
        loop(1, NZ, lambda i: w5_copy(i).start())

    def w_step6():
        loop(1, NZ, lambda i: w5_arrival(rem(z + i, NZ)).wait_recv())
        w5r[z] = w5s[...]
        for k in range(NZ):
            w6s[(k // 2) * 8:(k // 2) * 8 + 8, (k % 2) * TILE:(k % 2) * TILE + TILE] = w5r[k]
        loop(1, NREP, lambda i: w6_copy(i).start())

    def w_step7():
        loop(1, NREP, lambda i: w6_arrival(rem(rep + i, NREP)).wait_recv())
        w6r[rep] = w6s[...]
        for r in range(NREP):
            wgrad_ref[r * 32:(r + 1) * 32] = w6r[r] * (NBLK * NREP * 2 * TILE) ** -0.5

    def out_t(h, j):
        left_side = jnp.concatenate([gts[h][rows_ref[s, j]] for s in range(SLOT)], axis=1)
        return jnp.dot(left_side, dbuf[j], preferred_element_type=F32)

    def sib_copy(h, k):
        return remote(ss.at[h, k], sr.at[h, k], ss_send.at[h, k], ss_recv.at[h, k], sibling)

    def z_copy(h, d, m, xq):
        i = (d * 4 + m - 1) * 2 + xq
        dev = (jnp.where(d == 0, right[0], left[0]), rep)
        return remote(zs.at[h, i], zr.at[h, i], z_send.at[h, i], z_recv.at[h, i], dev)

    def z_arrival(h, d, m, xq):
        i = (d * 4 + m) * 2 + xq
        return remote(zs.at[h, i], zr.at[h, i], z_send.at[h, i], z_recv.at[h, i], right)

    def z_value(h, d, m, xq):
        return zr[h, (d * 4 + m) * 2 + xq].astype(F32)

    def x_copy(h, k):
        return remote(xs.at[h, k], xr.at[h, k], xf_send.at[h, k], xf_recv.at[h, k], xmate)

    def sib_term(h, d, m, xq):
        dz = m * (1 - 2 * d)
        k = rem(dz + 8, 8) * 2 + xq
        ss[h, k] = out_t(h, blkidx(dz, xq, 1)).astype(BF16)
        sib_copy(h, k).start()

    def own_term(h, d, m, xq):
        dz = m * (1 - 2 * d)
        zrel = rem(dz + 8, 8)
        k = zrel * 2 + xq
        value = out_t(h, blkidx(dz, xq, 0))
        sib_copy(h, k).wait_recv()
        value = value + sr[h, k].astype(F32)
        if h == 1 and xq == 0:
            x_copy(h, zrel).wait_recv()
            value = value + xr[h, zrel].astype(F32)
        return value

    def cross_term(d, m):
        zrel = rem(m * (1 - 2 * d) + 8, 8)
        xs[1, zrel] = own_term(1, d, m, 1).astype(BF16)
        x_copy(1, zrel).start()

    def start_on(h, d, m, xq):
        zs[h, (d * 4 + m - 1) * 2 + xq] = own_term(h, d, m, xq).astype(BF16)
        z_copy(h, d, m, xq).start()

    def pass_on(h, d, m, xq):
        value = own_term(h, d, m, xq)
        i = (d * 4 + m) * 2 + xq
        z_arrival(h, d, m, xq).wait_recv()
        zs[h, i - 2] = (value + zr[h, i].astype(F32)).astype(BF16)
        z_copy(h, d, m, xq).start()

    def arrive(h):
        loop(1, NREP, lambda i: g_arrival(h, rem(rep + i, NREP)).wait_recv())

    def open_0():
        arrive(0)
        loop(1, NREP, lambda i: w1_copy(rem(rep + i, NREP)).start())
        loop(0, 2, lambda q: sib_term(0, 0, 4, q))
        loop(0, 2, lambda q: sib_term(0, 1, 3, q))
        loop(0, 2, lambda q: start_on(0, 0, 4, q))
        loop(0, 2, lambda q: sib_term(0, 0, 3, q))
        loop(0, 2, lambda q: start_on(0, 1, 3, q))

    def open_1():
        arrive(1)
        loop(0, 2, lambda q: sib_term(1, 1, 4, 1 - q))
        loop(0, 4, lambda e: sib_term(1, rem(e, 2), 3, 1 - div(e, 2)))
        cross_term(1, 4)
        loop(0, 2, lambda d: cross_term(d, 3))
        loop(0, 4, lambda e: sib_term(1, rem(e, 2), 2, 1 - div(e, 2)))

    def third_0():
        def body(q):
            sib_term(0, 0, 2, q)
            sib_term(0, 1, 2, q)
            pass_on(0, 0, 3, q)

        loop(0, 2, body)

    def second_0():
        def body(e):
            d, q = rem(e, 2), div(e, 2)
            sib_term(0, d, 1, q)
            pass_on(0, d, 2, q)

        loop(0, 4, body)

    def first_0():
        loop(0, 2, lambda q: sib_term(0, 0, 0, q))
        loop(0, 4, lambda e: pass_on(0, rem(e, 2), 1, div(e, 2)))

    def third_1():
        loop(0, 2, lambda d: cross_term(d, 2))
        loop(0, 4, lambda e: sib_term(1, rem(e, 2), 1, 1 - div(e, 2)))
        start_on(1, 1, 4, 0)
        start_on(1, 0, 3, 0)

    def second_1():
        loop(0, 2, lambda d: cross_term(d, 1))
        loop(0, 2, lambda q: sib_term(1, 0, 0, 1 - q))
        pass_on(1, 1, 3, 0)

    def first_1():
        cross_term(0, 0)
        loop(0, 2, lambda d: pass_on(1, d, 2, 0))

    def last_1():
        loop(0, 2, lambda d: pass_on(1, d, 1, 0))

    def settled(h, xq):
        value = own_term(h, 0, 0, xq)
        z_arrival(h, 0, 0, xq).wait_recv()
        z_arrival(h, 1, 0, xq).wait_recv()
        return value + z_value(h, 0, 0, xq) + z_value(h, 1, 0, xq)

    def to_mate():
        xs[0, 0] = settled(0, 1).astype(BF16)
        x_copy(0, 0).start()

    def finish(h):
        value = settled(h, 0) + ngt[h].astype(F32)
        if h == 0:
            x_copy(0, 0).wait_recv()
            value = value + xr[0, 0].astype(F32)
        fgrad_ref[:, h * TILE:(h + 1) * TILE] = jnp.transpose(value).astype(BF16)

    def drain_forward(h):
        f_mate(h).wait_send()

        def near(e):
            k, xq = div(e, 2), rem(e, 2)
            f_right(h, blkidx(-k, xq, 0)).wait_send()
            f_left(h, blkidx(k, xq, 0)).wait_send()

        def farthest(xq):
            if h == 0:
                f_right(h, blkidx(-3, xq, 0)).wait_send()
            else:
                f_left(h, blkidx(3, xq, 0)).wait_send()

        loop(0, 6, near)
        loop(0, 2, farthest)
        loop(0, 16, lambda e: f_sib(h, blkidx(div(e, 2), rem(e, 2), 0)).wait_send())
        loop(1, NREP, lambda i: rs_copy(h, rem(rep + i, NREP)).wait_send())

    def drain_backward(h):
        cols = 2 - h

        def near(e):
            z_copy(h, rem(e, 2), 1 + div(e, 2 * cols), rem(div(e, 2), cols)).wait_send()

        loop(0, 6 * cols, near)
        loop(0, cols, lambda xq: z_copy(h, h, 4, xq).wait_send())
        loop(0, NZ if h else 1, lambda k: x_copy(h, k).wait_send())
        loop(0, 16, lambda e: sib_copy(h, e).wait_send())
        loop(1, NREP, lambda i: g_copy(h, i).wait_send())

    def drain_weight(i):
        r = rem(rep + i, NREP)
        dg_copy(r).wait_send()
        w1_copy(r).wait_send()
        w4_copy(i).wait_send()
        w5_copy(i).wait_send()
        w6_copy(i).wait_send()

    drain_forward(0)
    drain_forward(1)
    open_0()
    open_1()
    third_0()
    w_step2()
    third_1()
    second_0()
    w_step4()
    second_1()
    first_0()
    w_step5()
    first_1()
    to_mate()
    w_step6()
    last_1()
    drain_backward(0)
    drain_backward(1)
    finish(0)
    w_step7()
    finish(1)
    loop(1, NREP, drain_weight)
    for xq, cq in others:
        w2_copy(xq, cq).wait_send()


def place_kernel(a, b, c, out_a, out_b, out_c):
    out_a[...] = a[...]
    out_b[...] = b[...]
    out_c[...] = c[...]


def shards(node_features, weight, cotangent, tile_values, tile_rows, tile_cols, tile_count):
    half, width = TILE, 2 * TILE
    dma = pltpu.SemaphoreType.DMA
    vmem = pltpu.VMEM
    smem_spec = pl.BlockSpec(memory_space=pltpu.SMEM)
    vmem_spec = pl.BlockSpec(memory_space=pltpu.VMEM)
    any_spec = pl.BlockSpec(memory_space=pl.ANY)
    rows = tile_rows[0, 0].T
    outs = pl.pallas_call(
        layer_kernel,
        out_shape=[
            jax.ShapeDtypeStruct((width, width), BF16),
            jax.ShapeDtypeStruct((width, width), BF16),
            jax.ShapeDtypeStruct((width, width), F32),
        ],
        in_specs=[smem_spec] * 3 + [vmem_spec] + [any_spec] * 4,
        out_specs=[vmem_spec] * 3,
        scratch_shapes=[
            vmem((2, NBLK, width, half), BF16),
            vmem((NBLK, SLOT * TILE, width), BF16),
            vmem((NBLK, SLOT, TILE, TILE), jnp.int32),
            vmem((2, POS + 1, TILE, TILE), F32),
            vmem((POS + 1, 8, TILE), F32),
            vmem((8, POS), jnp.int32),
            pltpu.SMEM((8, POS), jnp.int32),
            vmem((width, width), BF16),
            vmem((width, width), BF16),
            vmem((2, NREP, width, half), BF16),
            vmem((2, NREP, width, half), BF16),
            vmem((2, width, half), F32),
            vmem((NREP, 2, 8, TILE), F32),
            vmem((NREP, 2, 8, TILE), F32),
            vmem((width, width), BF16),
            vmem((2, half, width), BF16),
            vmem((2 * NREP, half, TILE), BF16),
            vmem((2 * NREP, half, TILE), BF16),
            vmem((2, 16, half, width), BF16),
            vmem((2, 16, half, width), BF16),
            vmem((2, 16, half, width), BF16),
            vmem((2, 16, half, width), BF16),
            vmem((2, NZ, half, width), BF16),
            vmem((2, NZ, half, width), BF16),
            vmem((NREP, 32, width), BF16),
            vmem((NREP, 32, width), BF16),
            vmem((4, 32, width), F32),
            vmem((NZ, 8, TILE), F32),
            vmem((NZ, 8, TILE), F32),
            vmem((8, TILE), F32),
            vmem((NZ, 8, TILE), F32),
            vmem((32, width), F32),
            vmem((NREP, 32, width), F32),
            dma((4,)), dma((NBLK,)), dma,
            dma((2, NBLK)), dma((2, NBLK)), dma((2, NBLK)), dma((2, NBLK)), dma((2,)),
            dma((2, NREP)), dma((2, NREP)), dma((NREP,)), dma((NREP,)), dma((2, NREP)), dma((2, NREP)),
            dma((2, 16)), dma((2, 16)), dma((2, 16)), dma((2, 16)), dma((2, NZ)), dma((2, NZ)),
            dma((NREP,)), dma((NREP,)), dma((4,)), dma((4,)), dma((NZ,)), dma((NZ,)), dma((NZ,)), dma((NZ,)),
            dma((NREP,)), dma((NREP,)),
        ],
        compiler_params=pltpu.CompilerParams(
            collective_id=0, has_side_effects=True, vmem_limit_bytes=56 << 20),
        cost_estimate=pl.CostEstimate(flops=4 << 30, bytes_accessed=9 << 20, transcendentals=1 << 16),
        name="graph_layer",
    )(
        rows, tile_cols[0, 0].T, tile_count.reshape(-1), rows,
        node_features, weight, cotangent, tile_values[0, 0],
    )
    return pl.pallas_call(
        place_kernel,
        out_shape=[jax.ShapeDtypeStruct(out.shape, out.dtype) for out in outs],
        in_specs=[vmem_spec] * 3,
        out_specs=[vmem_spec] * 3,
        name="place",
    )(*outs)


def solution(mesh):
    in_specs = (
        P(("blk", "rep"), None),
        P(),
        P(("blk", "rep"), None),
        P("blk", "rep", None, None, None, None),
        P("blk", "rep", None, None),
        P("blk", "rep", None, None),
        P("blk", "rep", None),
    )
    out_specs = (P(("blk", "rep"), None), P(("blk", "rep"), None), P())
    return jax.shard_map(shards, mesh=mesh, in_specs=in_specs, out_specs=out_specs, check_vma=False)
```

```python
import jax
import jax.numpy as jnp
from jax import lax
from jax.experimental import pallas as pl
from jax.experimental.pallas import tpu as pltpu
from jax.sharding import PartitionSpec as P

TILE = 128
SLOT = 4
MESH = pl.DeviceIdType.MESH
F32 = jnp.float32
BF16 = jnp.bfloat16
NZ, NBLK, NREP, NX = 8, 32, 8, 2
POS = NBLK * SLOT


def rem(a, n):
    return lax.rem(a, jnp.int32(n))


def div(a, n):
    return lax.div(a, jnp.int32(n))


def loop(lo, hi, body):
    lax.fori_loop(lo, hi, lambda i, _: (body(i), 0)[1], 0)


def layer_kernel(
    rows_ref, cols_ref, count_ref, rowsv_ref, x_hbm, w_hbm, ct_hbm, tiles_hbm,
    act_ref, fgrad_ref, wgrad_ref,
    xbuf, dbuf, stage, sbuf, degs, idxv, idxs, wbuf, ctbuf,
    rs_src, rs_dst, own, deg_src, deg_dst, mixed, ngt, gt0, gt1,
    ss, sr, zs, zr, xs, xr,
    wp_src, wp_dst, w2g, w4s, w4r, w5s, w5r, w6s, w6r,
    in_sem, tile_sem, idx_sem,
    x_recv, xr_send, xl_send, xs_send, xx_send,
    rs_send, rs_recv, dg_send, dg_recv, g_send, g_recv,
    ss_send, ss_recv, z_send, z_recv, xf_send, xf_recv,
    w1_send, w1_recv, w2_send, w2_recv, w4_send, w4_recv, w5_send, w5_recv, w6_send, w6_recv,
):
    b = lax.axis_index("blk")
    rep = lax.axis_index("rep")
    z, xh, c = div(b, 4), rem(div(b, 2), 2), rem(b, 2)
    gts = (gt0, gt1)

    def blkidx(dz, xq, cq):
        return rem(z + dz + 8, 8) * 4 + rem(xh + xq, 2) * 2 + rem(c + cq, 2)

    def zdev(dz):
        return (blkidx(dz, 0, 0), rep)

    right, left = zdev(1), zdev(-1)
    sibling = (blkidx(0, 0, 1), rep)
    xmate = (blkidx(0, 1, 0), rep)

    def repdev(i):
        return (b, rem(rep + i, NREP))

    def remote(src, dst, send, recv, dev):
        return pltpu.make_async_remote_copy(
            src_ref=src, dst_ref=dst, send_sem=send, recv_sem=recv, device_id=dev, device_id_type=MESH)

    def own_load(h):
        return pltpu.make_async_copy(x_hbm.at[:, pl.ds(h * TILE, TILE)], xbuf.at[h, b], in_sem.at[h])

    def tile_load(p):
        zi, q = div(p, 4), rem(p, 4)
        return pltpu.make_async_copy(tiles_hbm.at[group_at(zi, q)], stage.at[p], tile_sem.at[p])

    def group_at(zi, q):
        odd = rem(zi, 2)
        dz = div(zi, 2) * (1 - 2 * odd) - odd
        return blkidx(dz, div(q, 2), rem(q, 2))

    w_load = pltpu.make_async_copy(w_hbm, wbuf, in_sem.at[2])
    ct_load = pltpu.make_async_copy(ct_hbm, ctbuf, in_sem.at[3])
    idx_copy = pltpu.make_async_copy(idxv, idxs, idx_sem)
    own_load(0).start()
    own_load(1).start()
    bar = pltpu.get_barrier_semaphore()
    for dev in (sibling, xmate, (blkidx(0, 1, 1), rep)):
        pl.semaphore_signal(bar, inc=1, device_id=dev, device_id_type=MESH)
    loop(1, NZ, lambda i: pl.semaphore_signal(bar, inc=1, device_id=zdev(i), device_id_type=MESH))
    loop(1, NREP, lambda i: pl.semaphore_signal(bar, inc=1, device_id=repdev(i), device_id_type=MESH))

    own_load(0).wait()
    own_load(1).wait()
    pl.semaphore_wait(bar, 17)

    def f_right(h, j):
        return remote(xbuf.at[h, j], xbuf.at[h, j], xr_send.at[h, j], x_recv.at[h, j], right)

    def f_left(h, j):
        return remote(xbuf.at[h, j], xbuf.at[h, j], xl_send.at[h, j], x_recv.at[h, j], left)

    def f_sib(h, j):
        return remote(xbuf.at[h, j], xbuf.at[h, j], xs_send.at[h, j], x_recv.at[h, j], sibling)

    def f_mate(h):
        return remote(xbuf.at[h, b], xbuf.at[h, b], xx_send.at[h], x_recv.at[h, b], xmate)

    def f_wait(h, j):
        f_sib(h, j).wait_recv()

    def start_own(h):
        f_right(h, b).start()
        f_left(h, b).start()
        f_sib(h, b).start()

    f_mate(0).start()
    f_mate(1).start()
    start_own(0)
    start_own(1)
    loop(0, NBLK, lambda p: tile_load(p).start())
    w_load.start()
    ct_load.start()

    def first_pos(j):
        cj, xj, zj = j & 1, (j >> 1) & 1, j >> 2
        dz = (zj - z + 8) & 7
        zi = jnp.where(dz < 4, 2 * dz, 15 - 2 * dz)
        q = ((xj + xh) & 1) * 2 + ((cj + c) & 1)
        return (zi * 4 + q) * SLOT

    idxv[...] = jnp.zeros((8, TILE), jnp.int32)
    idxv[0:SLOT, 0:NBLK] = rowsv_ref[...]
    group = lax.broadcasted_iota(jnp.int32, (NBLK, TILE), 0)
    lane = lax.broadcasted_iota(jnp.int32, (NBLK, TILE), 1)
    group_pos, lane_pos = first_pos(group), first_pos(lane & (NBLK - 1))
    row_l = [jnp.broadcast_to(idxv[s:s + 1, :], (TILE, TILE)) for s in range(SLOT)]
    row_s = [jnp.transpose(row)[0:NBLK] for row in row_l]
    last = jnp.full((NBLK, TILE), -1, jnp.int32)
    for t in range(SLOT):
        last = jnp.maximum(last, jnp.where(row_s[t] == lane, group_pos + t, -1))
    last = jnp.max(last, axis=0, keepdims=True)
    for s in range(SLOT):
        prev = jnp.full((NBLK, TILE), -1, jnp.int32)
        for t in range(SLOT):
            before = (row_s[t] == row_l[s][0:NBLK]) & (group_pos + t < lane_pos + s)
            prev = jnp.maximum(prev, jnp.where(before, group_pos + t, -1))
        prev = jnp.max(prev, axis=0, keepdims=True)
        idxv[s:s + 1, :] = jnp.where(prev < 0, POS, prev)
    idxv[SLOT:SLOT + 1, :] = jnp.where(last < 0, POS, last)
    idx_copy.start()
    for h in range(2):
        sbuf[h, POS] = jnp.zeros((TILE, TILE), F32)
    degs[POS] = jnp.zeros((8, TILE), F32)


    def prep(p, j):
        tile_load(p).wait()
        for s in range(SLOT):
            live = s < count_ref[j]
            col = cols_ref[s, j]
            m0 = jnp.where(live & (col == 0), 1.0, 0.0).astype(F32)
            m1 = jnp.where(live & (col == 1), 1.0, 0.0).astype(F32)
            tile = stage[p, s].astype(F32)
            dbuf[j, pl.ds(s * TILE, TILE), 0:TILE] = (tile * m0).astype(BF16)
            dbuf[j, pl.ds(s * TILE, TILE), TILE:2 * TILE] = (tile * m1).astype(BF16)
        ones = jnp.ones((16, 2 * TILE), BF16)
        sums = lax.dot_general(ones, dbuf[j], (((1,), (1,)), ((), ())), preferred_element_type=F32)
        for s in range(SLOT):
            degs[p * SLOT + s] = sums[0:8, s * TILE:(s + 1) * TILE] + degs[idxs[s, j]]

    def process(h, p):
        zi, q = div(p, 4), rem(p, 4)
        j = group_at(zi, q)
        pl.when(rem(q, 2) == 1)(lambda: f_wait(h, j))
        if h == 0:
            prep(p, j)
        prod = jnp.dot(dbuf[j], xbuf[h, j], preferred_element_type=F32)
        for s in range(SLOT):
            sbuf[h, p * SLOT + s] = prod[s * TILE:(s + 1) * TILE] + sbuf[h, idxs[s, j]]

    def rs_copy(h, r):
        return remote(rs_src.at[h, r], rs_dst.at[h, rep], rs_send.at[h, r], rs_recv.at[h, rep], (b, r))

    def rs_arrival(h, r):
        return remote(rs_src.at[h, r], rs_dst.at[h, r], rs_send.at[h, r], rs_recv.at[h, r], (b, r))

    def dg_copy(r):
        return remote(deg_src.at[r], deg_dst.at[rep], dg_send.at[r], dg_recv.at[rep], (b, r))

    def dg_arrival(r):
        return remote(deg_src.at[r], deg_dst.at[r], dg_send.at[r], dg_recv.at[r], (b, r))

    def forward_open(h):
        jx = blkidx(0, 1, 0)
        f_wait(h, jx)
        f_right(h, jx).start()
        f_left(h, jx).start()
        f_sib(h, jx).start()

    def forward_step(h, k):
        far_r, far_l = 4 - h, 3 + h

        def event(v):
            sgn, xq = rem(v, 2), div(v, 2)
            j = blkidx(k * (2 * sgn - 1), xq, 0)
            f_wait(h, j)
            if k < far_r:
                pl.when(sgn == 0)(lambda: f_right(h, j).start())
            if k < far_l:
                pl.when(sgn == 1)(lambda: f_left(h, j).start())
            f_sib(h, j).start()
            n = 1 if k == 1 else 2
            p0 = v if k == 1 else 4 + (k - 2) * 8 + v * 2
            loop(p0, p0 + n, lambda p: process(h, p))

        loop(0, 4, event)

    def forward_close(h):
        def far(xq):
            j = blkidx(4, xq, 0)
            f_wait(h, j)
            f_sib(h, j).start()
            loop(20 + xq * 4, 24 + xq * 4, lambda p: process(h, p))

        loop(0, 2, far)
        loop(28, 32, lambda p: process(h, p))

    def send_sums(h):
        def chunk(i):
            r = rem(rep + i, NREP)
            for t in range(2):
                rs_src[h, r, pl.ds(t * TILE, TILE)] = sbuf[h, idxs[SLOT, 2 * r + t]].astype(BF16)
            rs_copy(h, r).start()
            if h == 0:
                for t in range(2):
                    deg_src[r, t] = degs[idxs[SLOT, 2 * r + t]]
                dg_copy(r).start()

        loop(1, NREP, chunk)
        for t in range(2):
            own[h, pl.ds(t * TILE, TILE)] = sbuf[h, idxs[SLOT, 2 * rep + t]]
            if h == 0:
                deg_src[rep, t] = degs[idxs[SLOT, 2 * rep + t]]

    forward_open(0)
    forward_open(1)
    idx_copy.wait()
    for k in range(1, 4):
        forward_step(0, k)
        if k > 1:
            forward_step(1, k - 1)
    forward_close(0)
    send_sums(0)
    forward_step(1, 3)
    forward_close(1)
    send_sums(1)

    w_load.wait()
    ct_load.wait()
    loop(1, NREP, lambda i: dg_arrival(rem(rep + i, NREP)).wait_recv())
    deg = deg_src[rep]
    for i in range(1, NREP):
        deg = deg + deg_dst[rem(rep + i, NREP)]
    scale = lax.rsqrt(deg + 1.0)
    scale_row = jnp.concatenate([scale[0, 0:1], scale[1, 0:1]], axis=1)
    scale_col = [jnp.transpose(jnp.broadcast_to(scale[t, 0:1], (TILE, TILE))) for t in range(2)]
    for h in range(2):
        def add(i):
            r = rem(rep + i, NREP)
            rs_arrival(h, r).wait_recv()
            own[h] += rs_dst[h, r].astype(F32)

        loop(1, NREP, add)
        for t in range(2):
            part = own[h, pl.ds(t * TILE, TILE)] + xbuf[h, b, pl.ds(t * TILE, TILE)].astype(F32)
            mixed[pl.ds(t * TILE, TILE), h * TILE:(h + 1) * TILE] = (part * scale_col[t]).astype(BF16)
    pre = jnp.dot(mixed[...], wbuf[...], preferred_element_type=F32)
    sig = 1.0 / (1.0 + jnp.exp(-pre))
    act_grad = (ctbuf[...].astype(F32) * sig * (1.0 + pre * (1.0 - sig))).astype(BF16)

    def g_copy(h, i):
        mine = gts[h].at[pl.ds(2 * rep, 2)]
        return remote(mine, mine, g_send.at[h, i], g_recv.at[h, rep], repdev(i))

    def g_arrival(h, r):
        part = gts[h].at[pl.ds(2 * r, 2)]
        return remote(part, part, g_send.at[h, 0], g_recv.at[h, r], (b, r))

    for h in range(2):
        back = lax.dot_general(
            wbuf[h * TILE:(h + 1) * TILE, :], act_grad, (((1,), (1,)), ((), ())), preferred_element_type=F32)
        grad = (back * scale_row).astype(BF16)
        ngt[h] = grad
        for t in range(2):
            gts[h][2 * rep + t] = grad[:, t * TILE:(t + 1) * TILE]
        loop(1, NREP, lambda i: g_copy(h, i).start())

    def w1_copy(r):
        return remote(wp_src.at[r], wp_dst.at[rep], w1_send.at[r], w1_recv.at[rep], (b, r))

    def w1_arrival(r):
        return remote(wp_src.at[r], wp_dst.at[r], w1_send.at[r], w1_recv.at[r], (b, r))

    quad = xh * 2 + c
    others = ((0, 1), (1, 0), (1, 1))

    def w2_copy(xq, cq):
        return remote(w2g.at[quad], w2g.at[quad], w2_send.at[xq * 2 + cq], w2_recv.at[quad], (blkidx(0, xq, cq), rep))

    def w2_arrival(xq, cq):
        i = rem(xh + xq, 2) * 2 + rem(c + cq, 2)
        return remote(w2g.at[i], w2g.at[i], w2_send.at[0], w2_recv.at[i], sibling)

    def w4_copy(i):
        zz = rem(z + i, NZ)
        return remote(w4s.at[zz], w4r.at[z], w4_send.at[zz], w4_recv.at[z], zdev(i))

    def w4_arrival(zz):
        return remote(w4s.at[zz], w4r.at[zz], w4_send.at[zz], w4_recv.at[zz], right)

    def w5_copy(i):
        return remote(w5s, w5r.at[z], w5_send.at[i], w5_recv.at[z], zdev(i))

    def w5_arrival(zz):
        return remote(w5s, w5r.at[zz], w5_send.at[0], w5_recv.at[zz], right)

    def w6_copy(i):
        return remote(w6s, w6r.at[rep], w6_send.at[i], w6_recv.at[rep], repdev(i))

    def w6_arrival(r):
        return remote(w6s, w6r.at[r], w6_send.at[0], w6_recv.at[r], (b, r))

    act_ref[...] = (pre * sig).astype(BF16)
    part = lax.dot_general(mixed[...], act_grad, (((0,), (0,)), ((), ())), preferred_element_type=F32)
    for r in range(NREP):
        wp_src[r] = part[r * 32:(r + 1) * 32].astype(BF16)

    def w_step2():
        loop(1, NREP, lambda i: w1_arrival(rem(rep + i, NREP)).wait_recv())
        wp_dst[rep] = wp_src[rep]
        w2g[quad] = sum(wp_dst[r].astype(F32) for r in range(NREP))
        for xq, cq in others:
            w2_copy(xq, cq).start()

    def w_step4():
        for xq, cq in others:
            w2_arrival(xq, cq).wait_recv()
        both = (w2g[0] + w2g[1]) + (w2g[2] + w2g[3])
        for k in range(NZ):
            w4s[k] = both[(k // 2) * 8:(k // 2) * 8 + 8, (k % 2) * TILE:(k % 2) * TILE + TILE]
        loop(1, NZ, lambda i: w4_copy(i).start())

    def w_step5():
        loop(1, NZ, lambda i: w4_arrival(rem(z + i, NZ)).wait_recv())
        w4r[z] = w4s[z]
        w5s[...] = sum(w4r[k] for k in range(NZ))
        loop(1, NZ, lambda i: w5_copy(i).start())

    def w_step6():
        loop(1, NZ, lambda i: w5_arrival(rem(z + i, NZ)).wait_recv())
        w5r[z] = w5s[...]
        for k in range(NZ):
            w6s[(k // 2) * 8:(k // 2) * 8 + 8, (k % 2) * TILE:(k % 2) * TILE + TILE] = w5r[k]
        loop(1, NREP, lambda i: w6_copy(i).start())

    def w_step7():
        loop(1, NREP, lambda i: w6_arrival(rem(rep + i, NREP)).wait_recv())
        w6r[rep] = w6s[...]
        for r in range(NREP):
            wgrad_ref[r * 32:(r + 1) * 32] = w6r[r] * (NBLK * NREP * 2 * TILE) ** -0.5

    def out_t(h, j):
        left_side = jnp.concatenate([gts[h][rows_ref[s, j]] for s in range(SLOT)], axis=1)
        return jnp.dot(left_side, dbuf[j], preferred_element_type=F32)

    def sib_copy(h, k):
        return remote(ss.at[h, k], sr.at[h, k], ss_send.at[h, k], ss_recv.at[h, k], sibling)

    def z_copy(h, d, m, xq):
        i = (d * 4 + m - 1) * 2 + xq
        dev = (jnp.where(d == 0, right[0], left[0]), rep)
        return remote(zs.at[h, i], zr.at[h, i], z_send.at[h, i], z_recv.at[h, i], dev)

    def z_arrival(h, d, m, xq):
        i = (d * 4 + m) * 2 + xq
        return remote(zs.at[h, i], zr.at[h, i], z_send.at[h, i], z_recv.at[h, i], right)

    def z_value(h, d, m, xq):
        return zr[h, (d * 4 + m) * 2 + xq].astype(F32)

    def x_copy(h, k):
        return remote(xs.at[h, k], xr.at[h, k], xf_send.at[h, k], xf_recv.at[h, k], xmate)

    def sib_term(h, d, m, xq):
        dz = m * (1 - 2 * d)
        k = rem(dz + 8, 8) * 2 + xq
        ss[h, k] = out_t(h, blkidx(dz, xq, 1)).astype(BF16)
        sib_copy(h, k).start()

    def own_term(h, d, m, xq):
        dz = m * (1 - 2 * d)
        zrel = rem(dz + 8, 8)
        k = zrel * 2 + xq
        value = out_t(h, blkidx(dz, xq, 0))
        sib_copy(h, k).wait_recv()
        value = value + sr[h, k].astype(F32)
        if h == 1 and xq == 0:
            x_copy(h, zrel).wait_recv()
            value = value + xr[h, zrel].astype(F32)
        return value

    def cross_term(d, m):
        zrel = rem(m * (1 - 2 * d) + 8, 8)
        xs[1, zrel] = own_term(1, d, m, 1).astype(BF16)
        x_copy(1, zrel).start()

    def start_on(h, d, m, xq):
        zs[h, (d * 4 + m - 1) * 2 + xq] = own_term(h, d, m, xq).astype(BF16)
        z_copy(h, d, m, xq).start()

    def pass_on(h, d, m, xq):
        value = own_term(h, d, m, xq)
        i = (d * 4 + m) * 2 + xq
        z_arrival(h, d, m, xq).wait_recv()
        zs[h, i - 2] = (value + zr[h, i].astype(F32)).astype(BF16)
        z_copy(h, d, m, xq).start()

    def arrive(h):
        loop(1, NREP, lambda i: g_arrival(h, rem(rep + i, NREP)).wait_recv())

    def open_0():
        arrive(0)
        loop(1, NREP, lambda i: w1_copy(rem(rep + i, NREP)).start())
        loop(0, 2, lambda q: sib_term(0, 0, 4, q))
        loop(0, 2, lambda q: sib_term(0, 1, 3, q))
        loop(0, 2, lambda q: start_on(0, 0, 4, q))
        loop(0, 2, lambda q: sib_term(0, 0, 3, q))
        loop(0, 2, lambda q: start_on(0, 1, 3, q))

    def open_1():
        arrive(1)
        loop(0, 2, lambda q: sib_term(1, 1, 4, 1 - q))
        loop(0, 4, lambda e: sib_term(1, rem(e, 2), 3, 1 - div(e, 2)))
        cross_term(1, 4)
        loop(0, 2, lambda d: cross_term(d, 3))
        loop(0, 4, lambda e: sib_term(1, rem(e, 2), 2, 1 - div(e, 2)))

    def third_0():
        def body(q):
            pass_on(0, 0, 3, q)
            sib_term(0, 0, 2, q)
            sib_term(0, 1, 2, q)

        loop(0, 2, body)

    def second_0():
        def body(e):
            d, q = rem(e, 2), div(e, 2)
            pass_on(0, d, 2, q)
            sib_term(0, d, 1, q)

        loop(0, 4, body)

    def first_0():
        loop(0, 2, lambda q: sib_term(0, 0, 0, q))
        loop(0, 4, lambda e: pass_on(0, rem(e, 2), 1, div(e, 2)))

    def third_1():
        loop(0, 2, lambda d: cross_term(d, 2))
        loop(0, 4, lambda e: sib_term(1, rem(e, 2), 1, 1 - div(e, 2)))
        start_on(1, 1, 4, 0)
        start_on(1, 0, 3, 0)

    def second_1():
        loop(0, 2, lambda d: cross_term(d, 1))
        loop(0, 2, lambda q: sib_term(1, 0, 0, 1 - q))
        pass_on(1, 1, 3, 0)

    def first_1():
        loop(0, 2, lambda d: pass_on(1, d, 2, 0))
        cross_term(0, 0)

    def last_1():
        loop(0, 2, lambda d: pass_on(1, d, 1, 0))

    def settled(h, xq):
        value = own_term(h, 0, 0, xq)
        z_arrival(h, 0, 0, xq).wait_recv()
        z_arrival(h, 1, 0, xq).wait_recv()
        return value + z_value(h, 0, 0, xq) + z_value(h, 1, 0, xq)

    def to_mate():
        xs[0, 0] = settled(0, 1).astype(BF16)
        x_copy(0, 0).start()

    def finish(h):
        value = settled(h, 0) + ngt[h].astype(F32)
        if h == 0:
            x_copy(0, 0).wait_recv()
            value = value + xr[0, 0].astype(F32)
        fgrad_ref[:, h * TILE:(h + 1) * TILE] = jnp.transpose(value).astype(BF16)

    def drain_forward(h):
        f_mate(h).wait_send()

        def near(e):
            k, xq = div(e, 2), rem(e, 2)
            f_right(h, blkidx(-k, xq, 0)).wait_send()
            f_left(h, blkidx(k, xq, 0)).wait_send()

        def farthest(xq):
            if h == 0:
                f_right(h, blkidx(-3, xq, 0)).wait_send()
            else:
                f_left(h, blkidx(3, xq, 0)).wait_send()

        loop(0, 6, near)
        loop(0, 2, farthest)
        loop(0, 16, lambda e: f_sib(h, blkidx(div(e, 2), rem(e, 2), 0)).wait_send())
        loop(1, NREP, lambda i: rs_copy(h, rem(rep + i, NREP)).wait_send())

    def drain_backward(h):
        cols = 2 - h

        def near(e):
            z_copy(h, rem(e, 2), 1 + div(e, 2 * cols), rem(div(e, 2), cols)).wait_send()

        loop(0, 6 * cols, near)
        loop(0, cols, lambda xq: z_copy(h, h, 4, xq).wait_send())
        loop(0, NZ if h else 1, lambda k: x_copy(h, k).wait_send())
        loop(0, 16, lambda e: sib_copy(h, e).wait_send())
        loop(1, NREP, lambda i: g_copy(h, i).wait_send())

    def drain_weight(i):
        r = rem(rep + i, NREP)
        dg_copy(r).wait_send()
        w1_copy(r).wait_send()
        w4_copy(i).wait_send()
        w5_copy(i).wait_send()
        w6_copy(i).wait_send()

    drain_forward(0)
    drain_forward(1)
    open_0()
    open_1()
    third_0()
    w_step2()
    third_1()
    second_0()
    w_step4()
    second_1()
    first_0()
    w_step5()
    first_1()
    to_mate()
    w_step6()
    last_1()
    drain_backward(0)
    drain_backward(1)
    finish(0)
    w_step7()
    finish(1)
    loop(1, NREP, drain_weight)
    for xq, cq in others:
        w2_copy(xq, cq).wait_send()


def place_kernel(a, b, c, out_a, out_b, out_c):
    out_a[...] = a[...]
    out_b[...] = b[...]
    out_c[...] = c[...]


def shards(node_features, weight, cotangent, tile_values, tile_rows, tile_cols, tile_count):
    half, width = TILE, 2 * TILE
    dma = pltpu.SemaphoreType.DMA
    vmem = pltpu.VMEM
    smem_spec = pl.BlockSpec(memory_space=pltpu.SMEM)
    vmem_spec = pl.BlockSpec(memory_space=pltpu.VMEM)
    any_spec = pl.BlockSpec(memory_space=pl.ANY)
    rows = tile_rows[0, 0].T
    outs = pl.pallas_call(
        layer_kernel,
        out_shape=[
            jax.ShapeDtypeStruct((width, width), BF16),
            jax.ShapeDtypeStruct((width, width), BF16),
            jax.ShapeDtypeStruct((width, width), F32),
        ],
        in_specs=[smem_spec] * 3 + [vmem_spec] + [any_spec] * 4,
        out_specs=[vmem_spec] * 3,
        scratch_shapes=[
            vmem((2, NBLK, width, half), BF16),
            vmem((NBLK, SLOT * TILE, width), BF16),
            vmem((NBLK, SLOT, TILE, TILE), jnp.int32),
            vmem((2, POS + 1, TILE, TILE), F32),
            vmem((POS + 1, 8, TILE), F32),
            vmem((8, POS), jnp.int32),
            pltpu.SMEM((8, POS), jnp.int32),
            vmem((width, width), BF16),
            vmem((width, width), BF16),
            vmem((2, NREP, width, half), BF16),
            vmem((2, NREP, width, half), BF16),
            vmem((2, width, half), F32),
            vmem((NREP, 2, 8, TILE), F32),
            vmem((NREP, 2, 8, TILE), F32),
            vmem((width, width), BF16),
            vmem((2, half, width), BF16),
            vmem((2 * NREP, half, TILE), BF16),
            vmem((2 * NREP, half, TILE), BF16),
            vmem((2, 16, half, width), BF16),
            vmem((2, 16, half, width), BF16),
            vmem((2, 16, half, width), BF16),
            vmem((2, 16, half, width), BF16),
            vmem((2, NZ, half, width), BF16),
            vmem((2, NZ, half, width), BF16),
            vmem((NREP, 32, width), BF16),
            vmem((NREP, 32, width), BF16),
            vmem((4, 32, width), F32),
            vmem((NZ, 8, TILE), F32),
            vmem((NZ, 8, TILE), F32),
            vmem((8, TILE), F32),
            vmem((NZ, 8, TILE), F32),
            vmem((32, width), F32),
            vmem((NREP, 32, width), F32),
            dma((4,)), dma((NBLK,)), dma,
            dma((2, NBLK)), dma((2, NBLK)), dma((2, NBLK)), dma((2, NBLK)), dma((2,)),
            dma((2, NREP)), dma((2, NREP)), dma((NREP,)), dma((NREP,)), dma((2, NREP)), dma((2, NREP)),
            dma((2, 16)), dma((2, 16)), dma((2, 16)), dma((2, 16)), dma((2, NZ)), dma((2, NZ)),
            dma((NREP,)), dma((NREP,)), dma((4,)), dma((4,)), dma((NZ,)), dma((NZ,)), dma((NZ,)), dma((NZ,)),
            dma((NREP,)), dma((NREP,)),
        ],
        compiler_params=pltpu.CompilerParams(
            collective_id=0, has_side_effects=True, vmem_limit_bytes=56 << 20),
        cost_estimate=pl.CostEstimate(flops=4 << 30, bytes_accessed=9 << 20, transcendentals=1 << 16),
        name="graph_layer",
    )(
        rows, tile_cols[0, 0].T, tile_count.reshape(-1), rows,
        node_features, weight, cotangent, tile_values[0, 0],
    )
    return pl.pallas_call(
        place_kernel,
        out_shape=[jax.ShapeDtypeStruct(out.shape, out.dtype) for out in outs],
        in_specs=[vmem_spec] * 3,
        out_specs=[vmem_spec] * 3,
        name="place",
    )(*outs)


def solution(mesh):
    in_specs = (
        P(("blk", "rep"), None),
        P(),
        P(("blk", "rep"), None),
        P("blk", "rep", None, None, None, None),
        P("blk", "rep", None, None),
        P("blk", "rep", None, None),
        P("blk", "rep", None),
    )
    out_specs = (P(("blk", "rep"), None), P(("blk", "rep"), None), P())
    return jax.shard_map(shards, mesh=mesh, in_specs=in_specs, out_specs=out_specs, check_vma=False)
```
